512 devices in a mesh: row: 32 (over z, y_lo, core), col: 16 (over x, y_hi).
Axes of the slice: x: 4, y: 8 (y_hi: 4, y_lo: 2; y = y_hi * 2 + y_lo), z: 8, core: 2. Of those that a mesh axis runs over, the one named last changes fastest.
Arguments:
- points: float32 [65536, 16], P(('row', 'col')), may hold values from -1.7 to 1.7
- lengths: float32 [16], replicated, may hold values from 0.6 to 1.6
- outscale: float32 [1], replicated, may hold values from 0.5 to 2
- jitter: float32 [65536], P(('row', 'col')), may hold values from 0.5 to 2
- solution: float32 [65536, 16], P(('row', 'col')), may hold values from -6 to 6
- residual: float32 [65536, 16], P(('row', 'col')), may hold values from -11.3 to 11.3
- direction: float32 [65536, 16], P(('row', 'col')), may hold values from -11.3 to 11.3
Outputs:
- new_solution: float32 [65536, 16], P(('row', 'col'))
- new_residual: float32 [65536, 16], P(('row', 'col'))
- new_direction: float32 [65536, 16], P(('row', 'col'))
The draws below stay inside these ranges and needn't reach their ends.
All inputs are finite; a program needn't handle non-finite values.
Results may differ from the reference program's by a relative error of at most 0.000098.
Values sent between devices are 32-bit elements; how exact they have to be, the bound alone decides.
A program may use at most 64 MiB of HBM per device.

```python
import math
import jax
import jax.numpy as jnp
from jax import lax

D_IN = 16
NVEC = 16
NPTS = 65536


def ramp_rows(base, key, lowest, rising):
    ramp = jnp.arange(NPTS, dtype=jnp.float32) / NPTS
    spread = jnp.exp(jax.random.uniform(key, (NPTS, 1), jnp.float32, -0.7, 0.7))
    return base * (lowest + rising * ramp)[:, None] * spread


def draw_points(key, part):
    key = jax.random.fold_in(key, 11)
    groups = max(NPTS // 64, 4)
    key_labels, key_centres, key_offsets = jax.random.split(key, 3)
    labels = jax.random.randint(key_labels, (NPTS,), 0, groups)
    centres = jax.random.uniform(key_centres, (groups, D_IN), jnp.float32, -1.25, 1.25)
    offsets = jnp.clip(0.25 * jax.random.normal(key_offsets, (NPTS, D_IN), jnp.float32), -0.45, 0.45)
    return centres[labels] + offsets


def draw_residual(key, part):
    key = jax.random.fold_in(key, 12)
    key_base, key_rows = jax.random.split(key, 2)
    base = jnp.clip(jax.random.normal(key_base, (NPTS, NVEC), jnp.float32), -4.0, 4.0)
    return ramp_rows(base, key_rows, 0.7, 0.7)


def draw_direction(key, part):
    key = jax.random.fold_in(key, 13)
    key_base, key_rows = jax.random.split(key, 2)
    base = jnp.clip(jax.random.normal(key_base, (NPTS, NVEC), jnp.float32), -4.0, 4.0)
    return ramp_rows(base, key_rows, 0.7, 0.7)


def level_of(stream_key, shape, pieces, least, high):
    loudness = 1.0
    for dim, parts in pieces:
        heights = jax.random.uniform(jax.random.fold_in(jax.random.fold_in(stream_key, 6), dim), (parts,), jnp.float32, least / len(pieces), high / len(pieces))
        loudness = loudness * jnp.repeat(jnp.exp(heights), shape[dim] // parts).reshape((-1,) + (1,) * (len(shape) - 1 - dim))
    return loudness


def noise(key, shape, scale, bound, cuts=(), kind=jnp.bfloat16):
    result = scale * jax.random.normal(key, shape, jnp.float32)
    if cuts:
        result = result * level_of(key, shape, cuts, -0.22, 0.18)
    return jnp.clip(result, -bound, bound).astype(kind)


def setup_inputs(seed: int = 0) -> dict:
    key_list = jax.random.split(jax.random.key(seed), 8)
    return {
        "points": draw_points(jax.random.fold_in(key_list[7], 71), 0),
        "lengths": jnp.clip(jnp.exp(jax.random.uniform(key_list[1], (D_IN,), jnp.float32, math.log(0.6), math.log(1.6))), 0.6, 1.6),
        "outscale": jnp.clip(jnp.exp(jax.random.uniform(key_list[2], (1,), jnp.float32, math.log(0.5), math.log(2.0))), 0.5, 2.0),
        "jitter": jnp.clip(jnp.exp(math.log(2.0) - 1.3862944 * jax.random.uniform(key_list[3], (NPTS,), jnp.float32) ** level_of(key_list[3], (NPTS,), ((0, 512),), -0.2, 0.2)), 0.5, 2.0),
        "solution": noise(key_list[4], (NPTS, NVEC), 1.0, 6.0, ((0, 512),), jnp.float32),
        "residual": draw_residual(jax.random.fold_in(key_list[7], 71), 0),
        "direction": draw_direction(jax.random.fold_in(key_list[7], 71), 0),
    }


def kernel_times(block, block_sq, scaled, scaled_sq, direction, outscale):
    cross = jnp.dot(block, scaled.T, precision=lax.Precision.HIGHEST, preferred_element_type=jnp.float32)
    sqdist = block_sq[:, None] + scaled_sq[None, :] - 2.0 * cross
    kernel = outscale[0] * jnp.exp(-0.5 * sqdist)
    return jnp.dot(kernel, direction, precision=lax.Precision.HIGHEST, preferred_element_type=jnp.float32)


def reference(points, lengths, outscale, jitter, solution, residual, direction):
    scaled = points / lengths[None, :]
    scaled_sq = jnp.sum(scaled * scaled, axis=1)
    width = 512
    blocks_count = scaled.shape[0] // width if scaled.shape[0] % width == 0 else 1
    width = scaled.shape[0] // blocks_count
    blocks = scaled.reshape(blocks_count, width, scaled.shape[1])
    block_sqs = scaled_sq.reshape(blocks_count, width)

    def one_block(paired):
        return kernel_times(paired[0], paired[1], scaled, scaled_sq, direction, outscale)

    image = lax.map(one_block, (blocks, block_sqs)).reshape(direction.shape)
    image = image + jitter[:, None] * direction
    norm_now = jnp.sum(residual * residual, axis=0)
    curv = jnp.sum(direction * image, axis=0)
    alpha = norm_now / curv
    new_solution = solution + alpha[None, :] * direction
    new_residual = residual - alpha[None, :] * image
    norm_next = jnp.sum(new_residual * new_residual, axis=0)
    new_direction = new_residual + (norm_next / norm_now)[None, :] * direction
    return new_solution, new_residual, new_direction
```

```python
import math

import jax
import jax.numpy as jnp
from jax import lax
from jax.experimental import pallas as pl
from jax.experimental.pallas import tpu as pltpu
from jax.sharding import PartitionSpec as P

MESH = pl.DeviceIdType.MESH
BF = jnp.bfloat16
F32 = jnp.float32
LOG2E = math.log2(math.e)
DEPTH = 128
NEAR = 16
FAR = 32
SHARD = 128
NEAR_PTS = NEAR * SHARD
STEP = 512
STEPS = FAR * SHARD // STEP
SLOTS = STEP // SHARD


def split3(x):
    hi = x.astype(BF)
    rest = x - hi.astype(F32)
    mid = rest.astype(BF)
    low = (rest - mid.astype(F32)).astype(BF)
    return hi, mid, low


def augment(u, near):
    hi, mid, low = split3(u)
    half = -0.5 * jnp.sum(u * u, axis=0, keepdims=True)
    h0, h1, h2 = [part.astype(F32) for part in split3(half)]
    row = lax.broadcasted_iota(jnp.int32, u.shape, 0)
    if near:
        ones = jnp.where((row >= 3) & (row < 6), 1.0, 0.0)
        tail = jnp.where(row == 0, h0, jnp.where(row == 1, h1, jnp.where(row == 2, h2, ones)))
        parts = [hi, hi, mid, mid, hi, low]
    else:
        ones = jnp.where(row < 3, 1.0, 0.0)
        tail = jnp.where(row == 3, h0, jnp.where(row == 4, h1, jnp.where(row == 5, h2, ones)))
        parts = [hi, mid, hi, mid, low, hi]
    return jnp.concatenate(parts + [tail.astype(BF), jnp.zeros_like(hi)], axis=0)


def place():
    r, c = lax.axis_index("row"), lax.axis_index("col")
    x, z, core = c // 4, r // 4, lax.rem(r, 2)
    y = lax.rem(c, 4) * 2 + lax.rem(r // 2, 2)
    return x, y, z, core


def device(x, y, z, core):
    return (z * 4 + lax.rem(y, 2) * 2 + core, x * 4 + y // 2)


def kernel(
    points,
    lengths,
    outscale,
    jitter,
    sol,
    res,
    direction,
    new_sol,
    new_res,
    new_dir,
    near,
    far,
    near_op,
    far_op,
    dir_op,
    partial,
    landed,
    dots_near,
    dots_far,
    near_s,
    near_r,
    far_s,
    far_r,
    back_s,
    back_r,
    one_s,
    one_r,
    two_s,
    two_r,
):
    x, y, z, core = place()

    def near_peer(slot, sign):
        dx, dy = slot // 8, slot % 8
        dy = dy if sign > 0 else (8 - dy) % 8
        return device(lax.rem(x + 2 * dx, 4), lax.rem(y + dy, 8), z, core)

    def far_peer(q, dz):
        xl, co = q // 2, q % 2
        mate = x + xl * (1 - 2 * lax.rem(x, 2))
        return device(mate, y, lax.rem(z + dz, 8), lax.rem(core + co, 2))

    def send(src, dst, ss, rs, peer):
        return pltpu.make_async_remote_copy(
            src_ref=src, dst_ref=dst, send_sem=ss, recv_sem=rs, device_id=peer, device_id_type=MESH
        )

    near_to = [near_peer(s, 1) for s in range(NEAR)]
    near_from = [near_peer(s, -1) for s in range(NEAR)]
    far_to = [far_peer(q, dz) for q in range(4) for dz in range(8)]

    barrier = pltpu.get_barrier_semaphore()
    for peer in near_to[1:] + far_to[1:]:
        pl.semaphore_signal(barrier, inc=1, device_id=peer, device_id_type=MESH)

    eye = lax.broadcasted_iota(jnp.int32, (16, 16), 0) == lax.broadcasted_iota(jnp.int32, (16, 16), 1)
    column = jnp.sum(jnp.where(eye, jnp.broadcast_to(lengths[...], (16, 16)), 0.0), axis=1, keepdims=True)
    mine = points[...] * (math.sqrt(LOG2E) / column)
    near[0] = mine
    far[0, :16] = mine
    far[0, 16:] = direction[...]

    pl.semaphore_wait(barrier, NEAR + FAR - 2)

    order = (4, 3, 5, 2, 6, 1, 7)
    z_copy = {
        dz: send(far.at[0], far.at[dz], far_s.at[dz], far_r.at[dz], far_to[dz]) for dz in order
    }
    mate_copy = [
        send(far.at[dz], far.at[16 + dz], far_s.at[16 + dz], far_r.at[16 + dz], far_to[16]) for dz in range(8)
    ]
    core_copy = [
        send(far.at[k], far.at[k + 8], far_s.at[k + 8], far_r.at[k + 8], far_to[8])
        for k in list(range(8)) + list(range(16, 24))
    ]
    near_copy = [
        send(near.at[0], near.at[s], near_s.at[s], near_r.at[s], near_to[s]) for s in range(1, NEAR)
    ]
    for s in (12, 4, 11, 13, 3, 5, 10, 14, 2, 6, 9, 15, 8, 1, 7):
        near_copy[s - 1].start()
    for dz in order:
        z_copy[dz].start()
    mate_copy[0].start()
    core_copy[0].start()

    def prepare_near(s, carry):
        near_op[:, pl.ds(pl.multiple_of(s * SHARD, SHARD), SHARD)] = augment(near[s], True)
        return carry

    def prepare_far(k, carry):
        here = pl.ds(pl.multiple_of(k * SHARD, SHARD), SHARD)
        far_op[here, :] = augment(far[k, :16], False).T
        d = far[k, 16:]
        hi = d.astype(BF)
        dir_op[:, here] = jnp.concatenate([hi, (d - hi.astype(F32)).astype(BF)], axis=0)
        return carry

    for dz in reversed(order):
        z_copy[dz].wait_recv()
        mate_copy[dz].start()
        core_copy[dz].start()
    lax.fori_loop(0, 8, prepare_far, 0)
    for copy in near_copy:
        copy.wait_recv()
    lax.fori_loop(0, NEAR, prepare_near, 0)

    def step(t, carry):
        @pl.when(t == 2)
        def _():
            for k in range(8):
                core_copy[k].wait_recv()
                mate_copy[k].wait_recv()
                core_copy[8 + k].start()
            lax.fori_loop(8, 24, prepare_far, 0)

        @pl.when(t == 6)
        def _():
            for k in range(8):
                core_copy[8 + k].wait_recv()
            lax.fori_loop(24, 32, prepare_far, 0)

        here = pl.ds(pl.multiple_of(t * STEP, STEP), STEP)
        power = jnp.dot(far_op[here, :], near_op[...], preferred_element_type=F32)
        value = jnp.exp2(power)
        high = value.astype(BF)
        low = (value - high.astype(F32)).astype(BF)
        d = dir_op[:, here]
        a = jnp.dot(d, high, preferred_element_type=F32)
        b = jnp.dot(d[:16], low, preferred_element_type=F32)
        total = a[:16] + (a[16:] + b)
        for s in range(NEAR):
            piece = total[:, s * SHARD : (s + 1) * SHARD]
            partial[s] = jnp.where(t == 0, piece, partial[s] + piece)
        return carry

    lax.fori_loop(0, STEPS, step, 0)

    back_copy = [
        send(partial.at[s], landed.at[s], back_s.at[s], back_r.at[s], near_from[s]) for s in range(1, NEAR)
    ]
    for s in (12, 4, 11, 13, 3, 5, 10, 14, 2, 6, 9, 15, 8, 1, 7):
        back_copy[s - 1].start()
    image = partial[0]
    for s in range(1, NEAR):
        back_copy[s - 1].wait_recv()
        image = image + landed[s]
    d, r = direction[...], res[...]
    image = outscale[0] * image + jitter[...] * d
    terms = jnp.concatenate([r * r, d * image, r * image, image * image, jnp.zeros((64, SHARD), F32)], axis=0)
    dots_near[0:1, :] = jnp.sum(terms.T, axis=0, keepdims=True)
    one = [
        send(dots_near.at[pl.ds(0, 1)], dots_near.at[pl.ds(s, 1)], one_s.at[s], one_r.at[s], near_to[s])
        for s in range(1, NEAR)
    ]
    for s in (12, 4, 11, 13, 3, 5, 10, 14, 2, 6, 9, 15, 8, 1, 7):
        one[s - 1].start()
    for copy in one:
        copy.wait_recv()
    dots_far[0:1, :] = jnp.sum(dots_near[...], axis=0, keepdims=True)
    two = [
        send(dots_far.at[pl.ds(0, 1)], dots_far.at[pl.ds(s, 1)], two_s.at[s], two_r.at[s], far_to[s])
        for s in range(1, FAR)
    ]
    for s in range(1, FAR):
        two[s - 1].start()
    for copy in two:
        copy.wait_recv()
    sums = jnp.sum(dots_far[...], axis=0, keepdims=True)
    spread = jnp.broadcast_to(sums, (SHARD, SHARD)).T
    rr, dq, rq, qq = [spread[16 * k : 16 * (k + 1)] for k in range(4)]
    alpha = rr / dq
    next_rr = rr + alpha * (alpha * qq - 2.0 * rq)
    updated = r - alpha * image
    new_sol[...] = sol[...] + alpha * d
    new_res[...] = updated
    new_dir[...] = updated + (next_rr / rr) * d
    for copy in near_copy + list(z_copy.values()) + mate_copy + core_copy + back_copy + one + two:
        copy.wait_send()


def per_device(points, lengths, outscale, jitter, sol, res, direction):
    shape = jax.ShapeDtypeStruct((16, SHARD), F32)
    vmem = pl.BlockSpec(memory_space=pltpu.VMEM)
    dma = pltpu.SemaphoreType.DMA
    outs = pl.pallas_call(
        kernel,
        out_shape=(shape, shape, shape),
        in_specs=[vmem, vmem, pl.BlockSpec(memory_space=pltpu.SMEM), vmem, vmem, vmem, vmem],
        out_specs=(vmem, vmem, vmem),
        scratch_shapes=[
            pltpu.VMEM((NEAR, 16, SHARD), F32),
            pltpu.VMEM((FAR, 32, SHARD), F32),
            pltpu.VMEM((DEPTH, NEAR_PTS), BF),
            pltpu.VMEM((FAR * SHARD, DEPTH), BF),
            pltpu.VMEM((32, FAR * SHARD), BF),
            pltpu.VMEM((NEAR, 16, SHARD), F32),
            pltpu.VMEM((NEAR, 16, SHARD), F32),
            pltpu.VMEM((NEAR, SHARD), F32),
            pltpu.VMEM((FAR, SHARD), F32),
            dma((NEAR,)),
            dma((NEAR,)),
            dma((FAR,)),
            dma((FAR,)),
            dma((NEAR,)),
            dma((NEAR,)),
            dma((NEAR,)),
            dma((NEAR,)),
            dma((FAR,)),
            dma((FAR,)),
        ],
        compiler_params=pltpu.CompilerParams(
            collective_id=0, has_side_effects=True, vmem_limit_bytes=48 * 2**20
        ),
        name="cg_step",
    )(
        points.T,
        lengths.reshape(1, 16),
        outscale,
        jitter.reshape(1, SHARD),
        sol.T,
        res.T,
        direction.T,
    )
    return tuple(out.T for out in outs)


def solution(mesh):
    rows = P(("row", "col"), None)
    return jax.shard_map(
        per_device,
        mesh=mesh,
        in_specs=(rows, P(), P(), P(("row", "col")), rows, rows, rows),
        out_specs=(rows, rows, rows),
        check_vma=False,
    )
```

```python
import math

import jax
import jax.numpy as jnp
from jax import lax
from jax.experimental import pallas as pl
from jax.experimental.pallas import tpu as pltpu
from jax.sharding import PartitionSpec as P

MESH = pl.DeviceIdType.MESH
BF = jnp.bfloat16
F32 = jnp.float32
LOG2E = math.log2(math.e)
DEPTH = 128
NEAR = 16
FAR = 32
SHARD = 128
NEAR_PTS = NEAR * SHARD
CHUNK = 8
LEADERS = 32
DEVICES = 512
HALF = NEAR // 2
STEP = CHUNK * SHARD
WIDE = HALF * SHARD
OFFSETS = (
    (0, 0), (0, 1), (0, 7), (0, 2), (0, 6), (1, 0), (0, 3), (0, 5),
    (1, 1), (1, 7), (1, 2), (1, 6), (0, 4), (1, 3), (1, 5), (1, 4),
)


def split3(x):
    hi = x.astype(BF)
    rest = x - hi.astype(F32)
    mid = rest.astype(BF)
    low = (rest - mid.astype(F32)).astype(BF)
    return hi, mid, low


def augment(u, near):
    hi, mid, low = split3(u)
    half = -0.5 * jnp.sum(u * u, axis=0, keepdims=True)
    h0, h1, h2 = [part.astype(F32) for part in split3(half)]
    row = lax.broadcasted_iota(jnp.int32, u.shape, 0)
    if near:
        ones = jnp.where((row >= 3) & (row < 6), 1.0, 0.0)
        tail = jnp.where(row == 0, h0, jnp.where(row == 1, h1, jnp.where(row == 2, h2, ones)))
        parts = [hi, hi, mid, mid, hi, low]
    else:
        ones = jnp.where(row < 3, 1.0, 0.0)
        tail = jnp.where(row == 3, h0, jnp.where(row == 4, h1, jnp.where(row == 5, h2, ones)))
        parts = [hi, mid, hi, mid, low, hi]
    return jnp.concatenate(parts + [tail.astype(BF), jnp.zeros_like(hi)], axis=0)


def place():
    r, c = lax.axis_index("row"), lax.axis_index("col")
    x, z, core = c // 4, r // 4, lax.rem(r, 2)
    y = lax.rem(c, 4) * 2 + lax.rem(r // 2, 2)
    return x, y, z, core


def device(x, y, z, core):
    return (z * 4 + lax.rem(y, 2) * 2 + core, x * 4 + y // 2)


def kernel(
    points_hbm,
    lengths_hbm,
    outscale_hbm,
    jitter_hbm,
    res_hbm,
    direction_hbm,
    result,
    points,
    lengths,
    outscale,
    jitter,
    res,
    direction,
    load_sem,
    near,
    far,
    near_op,
    far_op,
    dir_op,
    partial,
    landed,
    dots,
    gathered,
    total,
    near_s,
    near_r,
    far_s,
    far_r,
    back_s,
    back_r,
    up_s,
    up_r,
    down_s,
    down_r,
):
    x, y, z, core = place()

    def near_peer(slot, sign):
        dx, dy = OFFSETS[slot]
        dy = dy if sign > 0 else (8 - dy) % 8
        return device(lax.rem(x + 2 * dx, 4), lax.rem(y + dy, 8), z, core)

    def far_peer(q, dz):
        xl, co = q // 2, q % 2
        mate = x + xl * (1 - 2 * lax.rem(x, 2))
        return device(mate, y, lax.rem(z + dz, 8), lax.rem(core + co, 2))

    def send(src, dst, ss, rs, peer):
        return pltpu.make_async_remote_copy(
            src_ref=src, dst_ref=dst, send_sem=ss, recv_sem=rs, device_id=peer, device_id_type=MESH
        )

    near_to = [near_peer(s, 1) for s in range(NEAR)]
    near_from = [near_peer(s, -1) for s in range(NEAR)]
    far_to = [far_peer(q, dz) for q in range(2) for dz in range(8)] + [far_peer(2, 0)]
    leader = (z == 0) & (core == 1)
    me = (z * 2 + core) * 32 + x * 8 + y

    barrier = pltpu.get_barrier_semaphore()
    for peer in near_to[1:] + far_to[1:]:
        pl.semaphore_signal(barrier, inc=1, device_id=peer, device_id_type=MESH)

    loads = [
        pltpu.make_async_copy(src, dst, load_sem.at[k])
        for k, (src, dst) in enumerate(
            (
                (points_hbm, points),
                (lengths_hbm, lengths),
                (direction_hbm, direction),
                (outscale_hbm, outscale),
                (jitter_hbm, jitter),
                (res_hbm, res),
            )
        )
    ]
    for load in loads:
        load.start()
    pending = []

    def go(copy):
        copy.start()
        pending.append(copy)

    for load in loads[:3]:
        load.wait()

    eye = lax.broadcasted_iota(jnp.int32, (16, 16), 0) == lax.broadcasted_iota(jnp.int32, (16, 16), 1)
    column = jnp.sum(jnp.where(eye, jnp.broadcast_to(lengths[...], (16, 16)), 0.0), axis=1, keepdims=True)
    mine = points[...] * (math.sqrt(LOG2E) / column)
    near[0] = mine
    far[0, :16] = mine
    far[0, 16:] = direction[...]

    pl.semaphore_wait(barrier, len(near_to) + len(far_to) - 2)

    order = (4, 3, 5, 2, 6, 1, 7)
    z_copy = {
        dz: send(far.at[0], far.at[dz], far_s.at[dz], far_r.at[dz], far_to[dz]) for dz in order
    }
    mate_copy = [
        send(far.at[dz], far.at[16 + dz], far_s.at[16 + dz], far_r.at[16 + dz], far_to[16]) for dz in range(8)
    ]
    core_copy = [
        send(far.at[k], far.at[k + 8], far_s.at[k + 8], far_r.at[k + 8], far_to[8])
        for k in list(range(8)) + list(range(16, 24))
    ]
    near_copy = [
        send(near.at[0], near.at[s], near_s.at[s], near_r.at[s], near_to[s]) for s in range(1, NEAR)
    ]
    for s in range(1, HALF):
        go(near_copy[s - 1])
    for dz in order:
        go(z_copy[dz])
    go(mate_copy[0])
    go(core_copy[0])
    for s in reversed(range(HALF, NEAR)):
        go(near_copy[s - 1])

    def prepare_near(s, carry):
        near_op[:, pl.ds(pl.multiple_of(s * SHARD, SHARD), SHARD)] = augment(near[s], True)
        return carry

    def prepare_far(k, carry):
        here = pl.ds(pl.multiple_of(k * SHARD, SHARD), SHARD)
        far_op[here, :] = augment(far[k, :16], False).T
        d = far[k, 16:]
        hi = d.astype(BF)
        dir_op[:, here] = jnp.concatenate([hi, (d - hi.astype(F32)).astype(BF)], axis=0)
        return carry

    for copy in near_copy[: HALF - 1]:
        copy.wait_recv()
    lax.fori_loop(0, HALF, prepare_near, 0)
    for dz in reversed(order):
        z_copy[dz].wait_recv()
        go(mate_copy[dz])
        go(core_copy[dz])
    lax.fori_loop(0, CHUNK, prepare_far, 0)

    back_copy = [
        send(partial.at[s], landed.at[s], back_s.at[s], back_r.at[s], near_from[s]) for s in range(1, NEAR)
    ]

    def step(t, carry):
        @pl.when(t == 1)
        def _():
            for copy in near_copy[HALF - 1 :]:
                copy.wait_recv()
            lax.fori_loop(HALF, NEAR, prepare_near, 0)

        @pl.when(t == 2)
        def _():
            for k in range(CHUNK):
                core_copy[k].wait_recv()
            lax.fori_loop(CHUNK, 2 * CHUNK, prepare_far, 0)

        @pl.when(t == 4)
        def _():
            for k in range(CHUNK):
                mate_copy[k].wait_recv()
                core_copy[CHUNK + k].start()
            lax.fori_loop(2 * CHUNK, 3 * CHUNK, prepare_far, 0)

        @pl.when(t == 5)
        def _():
            for k in range(CHUNK):
                core_copy[CHUNK + k].wait_recv()
            lax.fori_loop(3 * CHUNK, 4 * CHUNK, prepare_far, 0)

        @pl.when(t == 6)
        def _():
            for s in reversed(range(HALF, NEAR)):
                back_copy[s - 1].start()

        late = t // 4
        q = (1 - late) * (t // 2) + late * (2 + lax.rem(t, 2))
        h = (1 - late) * lax.rem(t, 2) + late * (3 - t // 2)
        rows = pl.ds(pl.multiple_of(q * STEP, STEP), STEP)
        columns = pl.ds(pl.multiple_of(h * WIDE, WIDE), WIDE)
        power = jnp.dot(far_op[rows, :], near_op[:, columns], preferred_element_type=F32)
        value = jnp.exp2(power)
        high = value.astype(BF)
        low = (value - high.astype(F32)).astype(BF)
        d = dir_op[:, rows]
        a = jnp.dot(d, high, preferred_element_type=F32)
        b = jnp.dot(d[:16], low, preferred_element_type=F32)
        product = a[:16] + (a[16:] + b)
        for s in range(HALF):
            piece = product[:, s * SHARD : (s + 1) * SHARD]
            slot = h * HALF + s
            partial[slot] = jnp.where(t < 2, piece, partial[slot] + piece)
        return carry

    lax.fori_loop(0, 8, step, 0)
    pending.extend(core_copy[CHUNK:] + back_copy[HALF - 1 :])
    for s in reversed(range(1, HALF)):
        go(back_copy[s - 1])
    image = partial[0]
    for s in range(1, NEAR):
        back_copy[s - 1].wait_recv()
        image = image + landed[s]
    for load in loads[3:]:
        load.wait()
    d, r = direction[...], res[...]
    image = outscale[0] * image + jitter[...] * d
    terms = jnp.concatenate([r * r, d * image, r * image, image * image, jnp.zeros((64, SHARD), F32)], axis=0)
    dots[0:1, :] = jnp.sum(terms.T, axis=0, keepdims=True)
    slot = gathered.at[pl.ds(me, 1)]
    row = dots.at[pl.ds(0, 1)]
    up = [
        send(row, slot, up_s.at[k], up_r, device(lax.rem(x + k // 8, 4), lax.rem(y + k % 8, 8), 0, 1))
        for k in range(LEADERS)
    ]
    for k in range(1, LEADERS):
        go(up[k])
    down = [
        send(total.at[pl.ds(0, 1)], total.at[pl.ds(0, 1)], down_s.at[k], down_r, device(x, y, k // 2, 1 - k % 2))
        for k in range(1, FAR // 2)
    ]

    @pl.when(leader)
    def _():
        own = pltpu.make_async_copy(row, slot, up_r)
        own.start()
        pltpu.make_async_copy(gathered, gathered, up_r).wait()
        total[0:1, :] = jnp.sum(gathered[...], axis=0, keepdims=True)
        for copy in down:
            copy.start()
        for copy in down:
            copy.wait_send()

    @pl.when(jnp.logical_not(leader))
    def _():
        up[0].start()
        down[0].wait_recv()
        up[0].wait_send()

    sums = total[0:1, :]
    spread = jnp.broadcast_to(sums, (SHARD, SHARD)).T
    rr, dq, rq, qq = [spread[16 * k : 16 * (k + 1)] for k in range(4)]
    alpha = rr / dq
    next_rr = rr + alpha * (alpha * qq - 2.0 * rq)
    result[0:16, :] = image
    result[16:32, :] = alpha
    result[32:48, :] = next_rr / rr
    for copy in pending:
        copy.wait_send()


def per_device(points, lengths, outscale, jitter, sol, res, direction):
    vmem = pl.BlockSpec(memory_space=pltpu.VMEM)
    dma = pltpu.SemaphoreType.DMA
    hbm = pl.BlockSpec(memory_space=pltpu.HBM)
    result = pl.pallas_call(
        kernel,
        out_shape=jax.ShapeDtypeStruct((48, SHARD), F32),
        in_specs=[hbm] * 6,
        out_specs=vmem,
        scratch_shapes=[
            pltpu.VMEM((16, SHARD), F32),
            pltpu.VMEM((1, 16), F32),
            pltpu.SMEM((1,), F32),
            pltpu.VMEM((1, SHARD), F32),
            pltpu.VMEM((16, SHARD), F32),
            pltpu.VMEM((16, SHARD), F32),
            dma((6,)),
            pltpu.VMEM((NEAR, 16, SHARD), F32),
            pltpu.VMEM((FAR, 32, SHARD), F32),
            pltpu.VMEM((DEPTH, NEAR_PTS), BF),
            pltpu.VMEM((FAR * SHARD, DEPTH), BF),
            pltpu.VMEM((32, FAR * SHARD), BF),
            pltpu.VMEM((NEAR, 16, SHARD), F32),
            pltpu.VMEM((NEAR, 16, SHARD), F32),
            pltpu.VMEM((8, SHARD), F32),
            pltpu.VMEM((DEVICES, SHARD), F32),
            pltpu.VMEM((8, SHARD), F32),
            dma((NEAR,)),
            dma((NEAR,)),
            dma((FAR,)),
            dma((FAR,)),
            dma((NEAR,)),
            dma((NEAR,)),
            dma((LEADERS,)),
            dma,
            dma((FAR // 2,)),
            dma,
        ],
        compiler_params=pltpu.CompilerParams(
            collective_id=0, has_side_effects=True, vmem_limit_bytes=63 * 2**20
        ),
        name="cg_step",
    )(
        points.T,
        lengths.reshape(1, 16),
        outscale,
        jitter.reshape(1, SHARD),
        res.T,
        direction.T,
    )
    image, alpha, beta = [result[16 * k : 16 * (k + 1)].T for k in range(3)]
    new_res = res - alpha * image
    return sol + alpha * direction, new_res, new_res + beta * direction


def solution(mesh):
    rows = P(("row", "col"), None)
    return jax.shard_map(
        per_device,
        mesh=mesh,
        in_specs=(rows, P(), P(), P(("row", "col")), rows, rows, rows),
        out_specs=(rows, rows, rows),
        check_vma=False,
    )
```

```python
import math

import jax
import jax.numpy as jnp
from jax import lax
from jax.experimental import pallas as pl
from jax.experimental.pallas import tpu as pltpu
from jax.sharding import PartitionSpec as P

MESH = pl.DeviceIdType.MESH
BF = jnp.bfloat16
F32 = jnp.float32
LOG2E = math.log2(math.e)
DEPTH = 128
NEAR = 16
FAR = 32
SHARD = 128
NEAR_PTS = NEAR * SHARD
CHUNK = 8
LEADERS = 32
DEVICES = 512
HALF = NEAR // 2
STEP = CHUNK * SHARD
WIDE = HALF * SHARD
NEAR_AT = (
    (0, 0), (1, 0), (7, 0), (0, 1), (1, 1), (7, 1), (2, 0), (6, 0),
    (3, 0), (5, 0), (2, 1), (6, 1), (4, 0), (3, 1), (5, 1), (4, 1),
)
FAR_AT = (
    (0, 0, 0), (0, 1, 0), (0, 3, 0), (1, 0, 0), (3, 0, 0), (0, 2, 0), (0, 0, 1), (0, 1, 1),
    (0, 3, 1), (0, 2, 1), (1, 0, 1), (3, 0, 1), (2, 0, 0), (2, 0, 1), (1, 1, 0), (3, 3, 0),
    (1, 3, 0), (3, 1, 0), (1, 2, 0), (3, 2, 0), (1, 1, 1), (3, 3, 1), (2, 1, 0), (2, 3, 0),
    (2, 2, 0), (1, 3, 1), (3, 1, 1), (1, 2, 1), (3, 2, 1), (2, 1, 1), (2, 3, 1), (2, 2, 1),
)
SLOT = {at: k for k, at in enumerate(FAR_AT)}
LINES = ((0, 1), (0, 3), (1, 0), (3, 0), (0, 2), (2, 0))

def split3(x):
    hi = x.astype(BF)
    rest = x - hi.astype(F32)
    mid = rest.astype(BF)
    low = (rest - mid.astype(F32)).astype(BF)
    return hi, mid, low


def augment(u, near):
    hi, mid, low = split3(u)
    half = -0.5 * jnp.sum(u * u, axis=0, keepdims=True)
    h0, h1, h2 = [part.astype(F32) for part in split3(half)]
    row = lax.broadcasted_iota(jnp.int32, u.shape, 0)
    if near:
        ones = jnp.where((row >= 3) & (row < 6), 1.0, 0.0)
        tail = jnp.where(row == 0, h0, jnp.where(row == 1, h1, jnp.where(row == 2, h2, ones)))
        parts = [hi, hi, mid, mid, hi, low]
    else:
        ones = jnp.where(row < 3, 1.0, 0.0)
        tail = jnp.where(row == 3, h0, jnp.where(row == 4, h1, jnp.where(row == 5, h2, ones)))
        parts = [hi, mid, hi, mid, low, hi]
    return jnp.concatenate(parts + [tail.astype(BF), jnp.zeros_like(hi)], axis=0)


def place():
    r, c = lax.axis_index("row"), lax.axis_index("col")
    x, z, core = c >> 2, r >> 2, r & 1
    y = (c & 3) * 2 + ((r >> 1) & 1)
    return x, y, z, core


def device(x, y, z, core):
    return (z * 4 + (y & 1) * 2 + core, x * 4 + (y >> 1))


def kernel(
    points_hbm,
    lengths_hbm,
    outscale_hbm,
    jitter_hbm,
    res_hbm,
    direction_hbm,
    result,
    points,
    lengths,
    outscale,
    jitter,
    res,
    direction,
    load_sem,
    near,
    far,
    near_op,
    far_op,
    dir_op,
    partial,
    landed,
    dots,
    gathered,
    total,
    near_s,
    near_r,
    far_s,
    far_r,
    back_s,
    back_r,
    up_s,
    up_r,
    down_s,
    down_r,
):
    x, y, z, core = place()

    def near_peer(slot, sign):
        dy, dz = NEAR_AT[slot]
        return device(x, (y + sign * dy) & 7, z ^ dz, core)

    def far_peer(a, b, c):
        return device((x + b) & 3, y, (z + 2 * a) & 7, core ^ c)

    def send(src, dst, ss, rs, peer):
        return pltpu.make_async_remote_copy(
            src_ref=src, dst_ref=dst, send_sem=ss, recv_sem=rs, device_id=peer, device_id_type=MESH
        )

    near_to = [near_peer(s, 1) for s in range(NEAR)]
    near_from = [near_peer(s, -1) for s in range(NEAR)]
    line_to = [far_peer(a, b, 0) for a, b in LINES]
    mate = far_peer(0, 0, 1)
    leader = (z == 0) & (core == 1)
    me = (z * 2 + core) * 32 + x * 8 + y

    barrier = pltpu.get_barrier_semaphore()
    greeted = line_to + near_to[:0:-1] + [mate]
    for peer in greeted:
        pl.semaphore_signal(barrier, inc=1, device_id=peer, device_id_type=MESH)

    loads = [
        pltpu.make_async_copy(src, dst, load_sem.at[k])
        for k, (src, dst) in enumerate(
            (
                (points_hbm, points),
                (lengths_hbm, lengths),
                (direction_hbm, direction),
                (outscale_hbm, outscale),
                (jitter_hbm, jitter),
                (res_hbm, res),
            )
        )
    ]
    for load in loads:
        load.start()
    pending = []

    def go(copy):
        copy.start()
        pending.append(copy)

    for load in loads[:3]:
        load.wait()

    eye = lax.broadcasted_iota(jnp.int32, (16, 16), 0) == lax.broadcasted_iota(jnp.int32, (16, 16), 1)
    column = jnp.sum(jnp.where(eye, jnp.broadcast_to(lengths[...], (16, 16)), 0.0), axis=1, keepdims=True)
    mine = points[...] * (math.sqrt(LOG2E) / column)
    near[0] = mine
    far[0, :16] = mine
    far[0, 16:] = direction[...]

    pl.semaphore_wait(barrier, len(greeted))

    def far_copy(source, at, peer):
        k = SLOT[at]
        return send(far.at[SLOT[source]], far.at[k], far_s.at[k], far_r.at[k], peer)

    line = {(a, b): far_copy((0, 0, 0), (a, b, 0), peer) for (a, b), peer in zip(LINES, line_to)}
    corner = {
        (a, b): far_copy((a, 0, 0), (a, b, 0), far_peer(0, b, 0)) for a in (1, 2, 3) for b in (1, 2, 3)
    }
    across = {(a, b): far_copy((a, b, 0), (a, b, 1), mate) for a in range(4) for b in range(4)}
    near_copy = [
        send(near.at[0], near.at[s], near_s.at[s], near_r.at[s], near_to[s]) for s in range(1, NEAR)
    ]
    for s in range(1, HALF):
        go(near_copy[s - 1])
    for at in LINES:
        go(line[at])
    go(across[0, 0])
    for s in reversed(range(HALF, NEAR)):
        go(near_copy[s - 1])

    def prepare_near(h):
        for s in range(h * HALF, h * HALF + HALF):
            near_op[:, s * SHARD : (s + 1) * SHARD] = augment(near[s], True)

    def prepare_far(q):
        for k in range(q * CHUNK, q * CHUNK + CHUNK):
            here = slice(k * SHARD, (k + 1) * SHARD)
            far_op[here, :] = augment(far[k, :16], False).T
            d = far[k, 16:]
            hi = d.astype(BF)
            dir_op[:, here] = jnp.concatenate([hi, (d - hi.astype(F32)).astype(BF)], axis=0)

    for copy in near_copy[: HALF - 1]:
        copy.wait_recv()
    prepare_near(0)
    for at in ((0, 1), (0, 3)):
        line[at].wait_recv()
        go(across[at])
    for at in ((1, 0), (3, 0)):
        line[at].wait_recv()
    for at in ((1, 1), (3, 3), (1, 3), (3, 1), (1, 2), (3, 2)):
        go(corner[at])
    for at in ((1, 0), (3, 0)):
        go(across[at])
    line[0, 2].wait_recv()
    go(across[0, 2])
    across[0, 0].wait_recv()
    across[0, 1].wait_recv()
    prepare_far(0)

    later = [corner[2, 1], corner[2, 3], corner[2, 2], across[2, 0]]
    back_copy = [
        send(partial.at[s], landed.at[s], back_s.at[s], back_r.at[s], near_from[s]) for s in range(1, NEAR)
    ]

    def step(t, carry):
        @pl.when(t == 1)
        def _():
            line[2, 0].wait_recv()
            for copy in later:
                copy.start()
            for copy in near_copy[HALF - 1 :]:
                copy.wait_recv()
            prepare_near(1)

        @pl.when(t == 2)
        def _():
            for at in ((1, 1), (3, 3)):
                corner[at].wait_recv()
                across[at].start()
            for at in ((0, 3), (0, 2), (1, 0), (3, 0), (2, 0)):
                across[at].wait_recv()
            prepare_far(1)

        @pl.when(t == 3)
        def _():
            for at in ((1, 3), (3, 1), (1, 2), (3, 2)):
                corner[at].wait_recv()
                across[at].start()

        @pl.when(t == 4)
        def _():
            for at in ((2, 1), (2, 3), (2, 2)):
                corner[at].wait_recv()
                across[at].start()
            for at in ((1, 1), (3, 3)):
                across[at].wait_recv()
            prepare_far(2)

        @pl.when(t == 5)
        def _():
            for a, b, c in FAR_AT[25:]:
                across[a, b].wait_recv()
            prepare_far(3)

        @pl.when(t == 6)
        def _():
            for s in reversed(range(HALF, NEAR)):
                back_copy[s - 1].start()

        late = t // 4
        q = (1 - late) * (t // 2) + late * (2 + lax.rem(t, 2))
        h = (1 - late) * lax.rem(t, 2) + late * (3 - t // 2)
        rows = pl.ds(pl.multiple_of(q * STEP, STEP), STEP)
        columns = pl.ds(pl.multiple_of(h * WIDE, WIDE), WIDE)
        power = jnp.dot(far_op[rows, :], near_op[:, columns], preferred_element_type=F32)
        value = jnp.exp2(power)
        high = value.astype(BF)
        low = (value - high.astype(F32)).astype(BF)
        d = dir_op[:, rows]
        a = jnp.dot(d, high, preferred_element_type=F32)
        b = jnp.dot(d[:16], low, preferred_element_type=F32)
        product = a[:16] + (a[16:] + b)
        for s in range(HALF):
            piece = product[:, s * SHARD : (s + 1) * SHARD]
            slot = h * HALF + s
            partial[slot] = jnp.where(t < 2, piece, partial[slot] + piece)
        return carry

    lax.fori_loop(0, 8, step, 0)
    pending.extend(later + [across[at] for at in corner] + back_copy[HALF - 1 :])
    for s in reversed(range(1, HALF)):
        go(back_copy[s - 1])
    image = partial[0]
    for s in range(1, NEAR):
        back_copy[s - 1].wait_recv()
        image = image + landed[s]
    for load in loads[3:]:
        load.wait()
    d, r = direction[...], res[...]
    image = outscale[0] * image + jitter[...] * d
    terms = jnp.concatenate([r * r, d * image, r * image, image * image, jnp.zeros((64, SHARD), F32)], axis=0)
    dots[0:1, :] = jnp.sum(terms.T, axis=0, keepdims=True)
    slot = gathered.at[pl.ds(me, 1)]
    row = dots.at[pl.ds(0, 1)]
    up = [
        send(row, slot, up_s.at[k], up_r, device((x + k // 8) & 3, (y + k % 8) & 7, 0, 1))
        for k in range(LEADERS)
    ]
    for k in range(1, LEADERS):
        go(up[k])
    down = [
        send(total.at[pl.ds(0, 1)], total.at[pl.ds(0, 1)], down_s.at[k], down_r, device(x, y, k // 2, 1 - k % 2))
        for k in range(1, FAR // 2)
    ]

    @pl.when(leader)
    def _():
        pltpu.make_async_copy(row, slot, up_r).start()

    @pl.when(jnp.logical_not(leader))
    def _():
        up[0].start()
        up[0].wait_send()

    for copy in pending:
        copy.wait_send()

    @pl.when(leader)
    def _():
        pltpu.make_async_copy(gathered, gathered, up_r).wait()
        total[0:1, :] = jnp.sum(gathered[...], axis=0, keepdims=True)
        for copy in down:
            copy.start()

    @pl.when(jnp.logical_not(leader))
    def _():
        down[0].wait_recv()

    sums = total[0:1, :]
    spread = jnp.broadcast_to(sums, (SHARD, SHARD)).T
    rr, dq, rq, qq = [spread[16 * k : 16 * (k + 1)] for k in range(4)]
    alpha = rr / dq
    next_rr = rr + alpha * (alpha * qq - 2.0 * rq)
    result[0:16, :] = image
    result[16:32, :] = alpha
    result[32:48, :] = next_rr / rr
    @pl.when(leader)
    def _():
        for copy in down:
            copy.wait_send()


def per_device(points, lengths, outscale, jitter, sol, res, direction):
    vmem = pl.BlockSpec(memory_space=pltpu.VMEM)
    dma = pltpu.SemaphoreType.DMA
    hbm = pl.BlockSpec(memory_space=pltpu.HBM)
    result = pl.pallas_call(
        kernel,
        out_shape=jax.ShapeDtypeStruct((48, SHARD), F32),
        in_specs=[hbm] * 6,
        out_specs=vmem,
        scratch_shapes=[
            pltpu.VMEM((16, SHARD), F32),
            pltpu.VMEM((1, 16), F32),
            pltpu.SMEM((1,), F32),
            pltpu.VMEM((1, SHARD), F32),
            pltpu.VMEM((16, SHARD), F32),
            pltpu.VMEM((16, SHARD), F32),
            dma((6,)),
            pltpu.VMEM((NEAR, 16, SHARD), F32),
            pltpu.VMEM((FAR, 32, SHARD), F32),
            pltpu.VMEM((DEPTH, NEAR_PTS), BF),
            pltpu.VMEM((FAR * SHARD, DEPTH), BF),
            pltpu.VMEM((32, FAR * SHARD), BF),
            pltpu.VMEM((NEAR, 16, SHARD), F32),
            pltpu.VMEM((NEAR, 16, SHARD), F32),
            pltpu.VMEM((8, SHARD), F32),
            pltpu.VMEM((DEVICES, SHARD), F32),
            pltpu.VMEM((8, SHARD), F32),
            dma((NEAR,)),
            dma((NEAR,)),
            dma((FAR,)),
            dma((FAR,)),
            dma((NEAR,)),
            dma((NEAR,)),
            dma((LEADERS,)),
            dma,
            dma((FAR // 2,)),
            dma,
        ],
        compiler_params=pltpu.CompilerParams(
            collective_id=0, has_side_effects=True, vmem_limit_bytes=63 * 2**20
        ),
        name="cg_step",
    )(
        points.T,
        lengths.reshape(1, 16),
        outscale,
        jitter.reshape(1, SHARD),
        res.T,
        direction.T,
    )
    image, alpha, beta = [result[16 * k : 16 * (k + 1)].T for k in range(3)]
    new_res = res - alpha * image
    return sol + alpha * direction, new_res, new_res + beta * direction


def solution(mesh):
    rows = P(("row", "col"), None)
    return jax.shard_map(
        per_device,
        mesh=mesh,
        in_specs=(rows, P(), P(), P(("row", "col")), rows, rows, rows),
        out_specs=(rows, rows, rows),
        check_vma=False,
    )
```

```python
import math

import jax
import jax.numpy as jnp
from jax import lax
from jax.experimental import pallas as pl
from jax.experimental.pallas import tpu as pltpu
from jax.sharding import PartitionSpec as P

MESH = pl.DeviceIdType.MESH
BF = jnp.bfloat16
F32 = jnp.float32
LOG2E = math.log2(math.e)
DEPTH = 128
NEAR = 16
FAR = 32
SHARD = 128
NEAR_PTS = NEAR * SHARD
CHUNK = 8
LEADERS = 32
DEVICES = 512
HALF = NEAR // 2
QUARTER = HALF // 2
STEP = CHUNK * SHARD
NEAR_AT = (
    (0, 0), (1, 0), (7, 0), (0, 1), (1, 1), (7, 1), (2, 0), (6, 0),
    (3, 0), (5, 0), (2, 1), (6, 1), (4, 0), (3, 1), (5, 1), (4, 1),
)
FAR_AT = (
    (0, 0, 0), (0, 1, 0), (0, 3, 0), (1, 0, 0), (3, 0, 0), (0, 2, 0), (0, 0, 1), (0, 1, 1),
    (0, 3, 1), (0, 2, 1), (1, 0, 1), (3, 0, 1), (2, 0, 0), (2, 0, 1), (1, 1, 0), (3, 3, 0),
    (1, 3, 0), (3, 1, 0), (1, 2, 0), (3, 2, 0), (1, 1, 1), (3, 3, 1), (2, 1, 0), (2, 3, 0),
    (2, 2, 0), (1, 3, 1), (3, 1, 1), (1, 2, 1), (3, 2, 1), (2, 1, 1), (2, 3, 1), (2, 2, 1),
)
SLOT = {at: k for k, at in enumerate(FAR_AT)}
LINES = ((0, 1), (0, 3), (1, 0), (3, 0), (0, 2), (2, 0))

def split3(x):
    hi = x.astype(BF)
    rest = x - hi.astype(F32)
    mid = rest.astype(BF)
    low = (rest - mid.astype(F32)).astype(BF)
    return hi, mid, low


def augment(u, near):
    hi, mid, low = split3(u)
    half = -0.5 * jnp.sum(u * u, axis=0, keepdims=True)
    h0, h1, h2 = [part.astype(F32) for part in split3(half)]
    row = lax.broadcasted_iota(jnp.int32, u.shape, 0)
    if near:
        ones = jnp.where((row >= 3) & (row < 6), 1.0, 0.0)
        tail = jnp.where(row == 0, h0, jnp.where(row == 1, h1, jnp.where(row == 2, h2, ones)))
        parts = [hi, hi, mid, mid, hi, low]
    else:
        ones = jnp.where(row < 3, 1.0, 0.0)
        tail = jnp.where(row == 3, h0, jnp.where(row == 4, h1, jnp.where(row == 5, h2, ones)))
        parts = [hi, mid, hi, mid, low, hi]
    return jnp.concatenate(parts + [tail.astype(BF), jnp.zeros_like(hi)], axis=0)


def place():
    r, c = lax.axis_index("row"), lax.axis_index("col")
    x, z, core = c >> 2, r >> 2, r & 1
    y = (c & 3) * 2 + ((r >> 1) & 1)
    return x, y, z, core


def device(x, y, z, core):
    return (z * 4 + (y & 1) * 2 + core, x * 4 + (y >> 1))


def kernel(
    points_hbm,
    lengths_hbm,
    outscale_hbm,
    jitter_hbm,
    res_hbm,
    direction_hbm,
    result,
    points,
    lengths,
    outscale,
    jitter,
    res,
    direction,
    load_sem,
    near,
    far,
    near_op,
    far_op,
    dir_op,
    partial,
    landed,
    dots,
    gathered,
    total,
    near_s,
    near_r,
    far_s,
    far_r,
    back_s,
    back_r,
    up_s,
    up_r,
    down_s,
    down_r,
):
    x, y, z, core = place()

    def near_peer(slot, sign):
        dy, dz = NEAR_AT[slot]
        return device(x, (y + sign * dy) & 7, z ^ dz, core)

    def far_peer(a, b, c):
        return device((x + b) & 3, y, (z + 2 * a) & 7, core ^ c)

    def send(src, dst, ss, rs, peer):
        return pltpu.make_async_remote_copy(
            src_ref=src, dst_ref=dst, send_sem=ss, recv_sem=rs, device_id=peer, device_id_type=MESH
        )

    near_to = [near_peer(s, 1) for s in range(NEAR)]
    near_from = [near_peer(s, -1) for s in range(NEAR)]
    line_to = [far_peer(a, b, 0) for a, b in LINES]
    mate = far_peer(0, 0, 1)
    leader = (z == 0) & (core == 1)
    me = (z * 2 + core) * 32 + x * 8 + y

    barrier = pltpu.get_barrier_semaphore()
    greeted = line_to + near_to[:0:-1] + [mate]
    for peer in greeted:
        pl.semaphore_signal(barrier, inc=1, device_id=peer, device_id_type=MESH)

    loads = [
        pltpu.make_async_copy(src, dst, load_sem.at[k])
        for k, (src, dst) in enumerate(
            (
                (points_hbm, points),
                (lengths_hbm, lengths),
                (direction_hbm, direction),
                (outscale_hbm, outscale),
                (jitter_hbm, jitter),
                (res_hbm, res),
            )
        )
    ]
    for load in loads:
        load.start()
    pending = []

    def go(copy):
        copy.start()
        pending.append(copy)

    for load in loads[:3]:
        load.wait()

    eye = lax.broadcasted_iota(jnp.int32, (16, 16), 0) == lax.broadcasted_iota(jnp.int32, (16, 16), 1)
    column = jnp.sum(jnp.where(eye, jnp.broadcast_to(lengths[...], (16, 16)), 0.0), axis=1, keepdims=True)
    mine = points[...] * (math.sqrt(LOG2E) / column)
    near[0] = mine
    far[0, :16] = mine
    far[0, 16:] = direction[...]

    pl.semaphore_wait(barrier, len(greeted))

    def far_copy(source, at, peer):
        k = SLOT[at]
        return send(far.at[SLOT[source]], far.at[k], far_s.at[k], far_r.at[k], peer)

    line = {(a, b): far_copy((0, 0, 0), (a, b, 0), peer) for (a, b), peer in zip(LINES, line_to)}
    corner = {
        (a, b): far_copy((a, 0, 0), (a, b, 0), far_peer(0, b, 0)) for a in (1, 2, 3) for b in (1, 2, 3)
    }
    across = {(a, b): far_copy((a, b, 0), (a, b, 1), mate) for a in range(4) for b in range(4)}
    near_copy = [
        send(near.at[0], near.at[s], near_s.at[s], near_r.at[s], near_to[s]) for s in range(1, NEAR)
    ]
    for s in range(1, HALF):
        go(near_copy[s - 1])
    for at in LINES:
        go(line[at])
    go(across[0, 0])
    for s in reversed(range(HALF, NEAR)):
        go(near_copy[s - 1])

    def prepare_near(h):
        for s in range(h * HALF, h * HALF + HALF):
            near_op[:, s * SHARD : (s + 1) * SHARD] = augment(near[s], True)

    def prepare_far(q):
        for k in range(q * CHUNK, q * CHUNK + CHUNK):
            here = slice(k * SHARD, (k + 1) * SHARD)
            far_op[here, :] = augment(far[k, :16], False).T
            d = far[k, 16:]
            hi = d.astype(BF)
            dir_op[:, here] = jnp.concatenate([hi, (d - hi.astype(F32)).astype(BF)], axis=0)

    for copy in near_copy[: HALF - 1]:
        copy.wait_recv()
    prepare_near(0)
    for at in ((0, 1), (0, 3)):
        line[at].wait_recv()
        go(across[at])
    for at in ((1, 0), (3, 0)):
        line[at].wait_recv()
    for at in ((1, 1), (3, 3), (1, 3), (3, 1), (1, 2), (3, 2)):
        go(corner[at])
    for at in ((1, 0), (3, 0)):
        go(across[at])
    line[0, 2].wait_recv()
    go(across[0, 2])
    across[0, 0].wait_recv()
    across[0, 1].wait_recv()
    prepare_far(0)

    later = [corner[2, 1], corner[2, 3], corner[2, 2], across[2, 0]]
    back_copy = [
        send(partial.at[s], landed.at[s], back_s.at[s], back_r.at[s], near_from[s]) for s in range(1, NEAR)
    ]

    def tile(q, slot, slots, fresh):
        rows = pl.ds(pl.multiple_of(q * STEP, STEP), STEP)
        columns = pl.ds(pl.multiple_of(slot * SHARD, slots * SHARD), slots * SHARD)
        power = jnp.dot(far_op[rows, :], near_op[:, columns], preferred_element_type=F32)
        value = jnp.exp2(power)
        high = value.astype(BF)
        low = (value - high.astype(F32)).astype(BF)
        d = dir_op[:, rows]
        a = jnp.dot(d, high, preferred_element_type=F32)
        b = jnp.dot(d[:16], low, preferred_element_type=F32)
        product = a[:16] + (a[16:] + b)
        for s in range(slots):
            piece = product[:, s * SHARD : (s + 1) * SHARD]
            partial[slot + s] = piece + (partial[slot + s] if fresh is False else jnp.where(fresh, 0.0, partial[slot + s]))

    def step(t, carry):
        @pl.when(t == 1)
        def _():
            line[2, 0].wait_recv()
            for copy in later:
                copy.start()
            for copy in near_copy[HALF - 1 :]:
                copy.wait_recv()
            prepare_near(1)

        @pl.when(t == 2)
        def _():
            for at in ((1, 1), (3, 3)):
                corner[at].wait_recv()
                across[at].start()
            for at in ((0, 3), (0, 2), (1, 0), (3, 0), (2, 0)):
                across[at].wait_recv()
            prepare_far(1)

        @pl.when(t == 3)
        def _():
            for at in ((1, 3), (3, 1), (1, 2), (3, 2)):
                corner[at].wait_recv()
                across[at].start()

        @pl.when(t == 4)
        def _():
            for at in ((2, 1), (2, 3), (2, 2)):
                corner[at].wait_recv()
                across[at].start()
            for at in ((1, 1), (3, 3)):
                across[at].wait_recv()
            prepare_far(2)

        @pl.when(t == 5)
        def _():
            for a, b, c in FAR_AT[25:]:
                across[a, b].wait_recv()
            prepare_far(3)

        @pl.when(t == 6)
        def _():
            for s in reversed(range(HALF, NEAR)):
                back_copy[s - 1].start()

        late = t // 4
        q = (1 - late) * (t // 2) + late * (2 + lax.rem(t, 2))
        h = (1 - late) * lax.rem(t, 2) + late * (3 - t // 2)
        tile(q, h * HALF, HALF, t < 2)
        return carry

    lax.fori_loop(0, 7, step, 0)
    for first in (QUARTER, 0):
        tile(3, first, QUARTER, False)
        for k in reversed(range(max(first, 1), first + QUARTER)):
            back_copy[k - 1].start()
    pending.extend(later + [across[at] for at in corner] + back_copy)
    image = partial[0]
    for s in range(1, NEAR):
        back_copy[s - 1].wait_recv()
        image = image + landed[s]
    for load in loads[3:]:
        load.wait()
    d, r = direction[...], res[...]
    image = outscale[0] * image + jitter[...] * d
    terms = jnp.concatenate([r * r, d * image, r * image, image * image, jnp.zeros((64, SHARD), F32)], axis=0)
    dots[0:1, :] = jnp.sum(terms.T, axis=0, keepdims=True)
    slot = gathered.at[pl.ds(me, 1)]
    row = dots.at[pl.ds(0, 1)]
    up = [
        send(row, slot, up_s.at[k], up_r, device((x + k // 8) & 3, (y + k % 8) & 7, 0, 1))
        for k in range(LEADERS)
    ]
    for k in range(1, LEADERS):
        go(up[k])
    down = [
        send(total.at[pl.ds(0, 1)], total.at[pl.ds(0, 1)], down_s.at[k], down_r, device(x, y, k // 2, 1 - k % 2))
        for k in range(1, FAR // 2)
    ]

    @pl.when(leader)
    def _():
        pltpu.make_async_copy(row, slot, up_r).start()

    @pl.when(jnp.logical_not(leader))
    def _():
        up[0].start()
        up[0].wait_send()

    for copy in pending:
        copy.wait_send()

    @pl.when(leader)
    def _():
        pltpu.make_async_copy(gathered, gathered, up_r).wait()
        total[0:1, :] = jnp.sum(gathered[...], axis=0, keepdims=True)
        for copy in down:
            copy.start()

    @pl.when(jnp.logical_not(leader))
    def _():
        down[0].wait_recv()

    sums = total[0:1, :]
    spread = jnp.broadcast_to(sums, (SHARD, SHARD)).T
    rr, dq, rq, qq = [spread[16 * k : 16 * (k + 1)] for k in range(4)]
    alpha = rr / dq
    next_rr = rr + alpha * (alpha * qq - 2.0 * rq)
    result[0:16, :] = image
    result[16:32, :] = alpha
    result[32:48, :] = next_rr / rr
    @pl.when(leader)
    def _():
        for copy in down:
            copy.wait_send()


def per_device(points, lengths, outscale, jitter, sol, res, direction):
    vmem = pl.BlockSpec(memory_space=pltpu.VMEM)
    dma = pltpu.SemaphoreType.DMA
    hbm = pl.BlockSpec(memory_space=pltpu.HBM)
    result = pl.pallas_call(
        kernel,
        out_shape=jax.ShapeDtypeStruct((48, SHARD), F32),
        in_specs=[hbm] * 6,
        out_specs=vmem,
        scratch_shapes=[
            pltpu.VMEM((16, SHARD), F32),
            pltpu.VMEM((1, 16), F32),
            pltpu.SMEM((1,), F32),
            pltpu.VMEM((1, SHARD), F32),
            pltpu.VMEM((16, SHARD), F32),
            pltpu.VMEM((16, SHARD), F32),
            dma((6,)),
            pltpu.VMEM((NEAR, 16, SHARD), F32),
            pltpu.VMEM((FAR, 32, SHARD), F32),
            pltpu.VMEM((DEPTH, NEAR_PTS), BF),
            pltpu.VMEM((FAR * SHARD, DEPTH), BF),
            pltpu.VMEM((32, FAR * SHARD), BF),
            pltpu.VMEM((NEAR, 16, SHARD), F32),
            pltpu.VMEM((NEAR, 16, SHARD), F32),
            pltpu.VMEM((8, SHARD), F32),
            pltpu.VMEM((DEVICES, SHARD), F32),
            pltpu.VMEM((8, SHARD), F32),
            dma((NEAR,)),
            dma((NEAR,)),
            dma((FAR,)),
            dma((FAR,)),
            dma((NEAR,)),
            dma((NEAR,)),
            dma((LEADERS,)),
            dma,
            dma((FAR // 2,)),
            dma,
        ],
        compiler_params=pltpu.CompilerParams(
            collective_id=0, has_side_effects=True, vmem_limit_bytes=63 * 2**20
        ),
        name="cg_step",
    )(
        points.T,
        lengths.reshape(1, 16),
        outscale,
        jitter.reshape(1, SHARD),
        res.T,
        direction.T,
    )
    image, alpha, beta = [result[16 * k : 16 * (k + 1)].T for k in range(3)]
    new_res = res - alpha * image
    return sol + alpha * direction, new_res, new_res + beta * direction


def solution(mesh):
    rows = P(("row", "col"), None)
    return jax.shard_map(
        per_device,
        mesh=mesh,
        in_specs=(rows, P(), P(), P(("row", "col")), rows, rows, rows),
        out_specs=(rows, rows, rows),
        check_vma=False,
    )
```

```python
import math

import jax
import jax.numpy as jnp
from jax import lax
from jax.experimental import pallas as pl
from jax.experimental.pallas import tpu as pltpu
from jax.sharding import PartitionSpec as P

MESH = pl.DeviceIdType.MESH
BF = jnp.bfloat16
F32 = jnp.float32
LOG2E = math.log2(math.e)
DEPTH = 128
NEAR = 16
FAR = 32
SHARD = 128
NEAR_PTS = NEAR * SHARD
CHUNK = 8
LEADERS = 32
DEVICES = 512
HALF = NEAR // 2
QUARTER = HALF // 2
STEP = CHUNK * SHARD
NEAR_AT = (
    (0, 0), (1, 0), (7, 0), (0, 1), (1, 1), (7, 1), (2, 0), (6, 0),
    (3, 0), (5, 0), (2, 1), (6, 1), (4, 0), (3, 1), (5, 1), (4, 1),
)
FAR_AT = (
    (0, 0, 0), (0, 1, 0), (0, 3, 0), (1, 0, 0), (3, 0, 0), (0, 2, 0), (0, 0, 1), (0, 1, 1),
    (0, 3, 1), (0, 2, 1), (1, 0, 1), (3, 0, 1), (2, 0, 0), (2, 0, 1), (1, 1, 0), (3, 3, 0),
    (1, 3, 0), (3, 1, 0), (1, 2, 0), (3, 2, 0), (1, 1, 1), (3, 3, 1), (2, 1, 0), (2, 3, 0),
    (2, 2, 0), (1, 3, 1), (3, 1, 1), (1, 2, 1), (3, 2, 1), (2, 1, 1), (2, 3, 1), (2, 2, 1),
)
SLOT = {at: k for k, at in enumerate(FAR_AT)}
LINES = ((0, 1), (0, 3), (1, 0), (3, 0), (0, 2), (2, 0))

def split3(x):
    hi = x.astype(BF)
    rest = x - hi.astype(F32)
    mid = rest.astype(BF)
    low = (rest - mid.astype(F32)).astype(BF)
    return hi, mid, low


def augment(u, near):
    hi, mid, low = split3(u)
    half = -0.5 * jnp.sum(u * u, axis=0, keepdims=True)
    h0, h1, h2 = [part.astype(F32) for part in split3(half)]
    row = lax.broadcasted_iota(jnp.int32, u.shape, 0)
    if near:
        ones = jnp.where((row >= 3) & (row < 6), 1.0, 0.0)
        tail = jnp.where(row == 0, h0, jnp.where(row == 1, h1, jnp.where(row == 2, h2, ones)))
        parts = [hi, hi, mid, mid, hi, low]
    else:
        ones = jnp.where(row < 3, 1.0, 0.0)
        tail = jnp.where(row == 3, h0, jnp.where(row == 4, h1, jnp.where(row == 5, h2, ones)))
        parts = [hi, mid, hi, mid, low, hi]
    return jnp.concatenate(parts + [tail.astype(BF), jnp.zeros_like(hi)], axis=0)


def place():
    r, c = lax.axis_index("row"), lax.axis_index("col")
    x, z, core = c >> 2, r >> 2, r & 1
    y = (c & 3) * 2 + ((r >> 1) & 1)
    return x, y, z, core


def device(x, y, z, core):
    return (z * 4 + (y & 1) * 2 + core, x * 4 + (y >> 1))


def kernel(
    points_hbm,
    lengths_hbm,
    outscale_hbm,
    jitter_hbm,
    res_hbm,
    direction_hbm,
    result,
    points,
    lengths,
    outscale,
    jitter,
    res,
    direction,
    load_sem,
    near,
    far,
    near_op,
    far_op,
    dir_op,
    partial,
    landed,
    dots,
    gathered,
    total,
    near_s,
    near_r,
    far_s,
    far_r,
    back_s,
    back_r,
    up_s,
    up_r,
    down_s,
    down_r,
):
    x, y, z, core = place()

    def near_peer(slot, sign):
        dy, dz = NEAR_AT[slot]
        return device(x, (y + sign * dy) & 7, z ^ dz, core)

    def far_peer(a, b, c):
        return device((x + b) & 3, y, (z + 2 * a) & 7, core ^ c)

    def send(src, dst, ss, rs, peer):
        return pltpu.make_async_remote_copy(
            src_ref=src, dst_ref=dst, send_sem=ss, recv_sem=rs, device_id=peer, device_id_type=MESH
        )

    near_to = [near_peer(s, 1) for s in range(NEAR)]
    near_from = [near_peer(s, -1) for s in range(NEAR)]
    line_to = [far_peer(a, b, 0) for a, b in LINES]
    mate = far_peer(0, 0, 1)
    leader = (z == 0) & (core == 1)
    me = (z * 2 + core) * 32 + x * 8 + y

    barrier = pltpu.get_barrier_semaphore()
    greeted = line_to + near_to[:0:-1] + [mate]
    for peer in greeted:
        pl.semaphore_signal(barrier, inc=1, device_id=peer, device_id_type=MESH)

    loads = [
        pltpu.make_async_copy(src, dst, load_sem.at[k])
        for k, (src, dst) in enumerate(
            (
                (points_hbm, points),
                (lengths_hbm, lengths),
                (direction_hbm, direction),
                (outscale_hbm, outscale),
                (jitter_hbm, jitter),
                (res_hbm, res),
            )
        )
    ]
    for load in loads:
        load.start()
    pending = []

    def go(copy):
        copy.start()
        pending.append(copy)

    for load in loads[:3]:
        load.wait()

    eye = lax.broadcasted_iota(jnp.int32, (16, 16), 0) == lax.broadcasted_iota(jnp.int32, (16, 16), 1)
    column = jnp.sum(jnp.where(eye, jnp.broadcast_to(lengths[...], (16, 16)), 0.0), axis=1, keepdims=True)
    mine = points[...] * (math.sqrt(LOG2E) / column)
    near[0] = mine
    far[0, :16] = mine
    far[0, 16:] = direction[...]

    pl.semaphore_wait(barrier, len(greeted))

    def far_copy(source, at, peer):
        k = SLOT[at]
        return send(far.at[SLOT[source]], far.at[k], far_s.at[k], far_r.at[k], peer)

    line = {(a, b): far_copy((0, 0, 0), (a, b, 0), peer) for (a, b), peer in zip(LINES, line_to)}
    corner = {
        (a, b): far_copy((a, 0, 0), (a, b, 0), far_peer(0, b, 0)) for a in (1, 2, 3) for b in (1, 2, 3)
    }
    across = {(a, b): far_copy((a, b, 0), (a, b, 1), mate) for a in range(4) for b in range(4)}
    near_copy = [
        send(near.at[0], near.at[s], near_s.at[s], near_r.at[s], near_to[s]) for s in range(1, NEAR)
    ]
    for s in range(1, HALF):
        go(near_copy[s - 1])
    for at in LINES:
        go(line[at])
    go(across[0, 0])
    for s in reversed(range(HALF, NEAR)):
        go(near_copy[s - 1])

    def prepare_near(h):
        for s in range(h * HALF, h * HALF + HALF):
            near_op[:, s * SHARD : (s + 1) * SHARD] = augment(near[s], True)

    def prepare_far(q):
        for k in range(q * CHUNK, q * CHUNK + CHUNK):
            here = slice(k * SHARD, (k + 1) * SHARD)
            far_op[here, :] = augment(far[k, :16], False).T
            d = far[k, 16:]
            hi = d.astype(BF)
            dir_op[:, here] = jnp.concatenate([hi, (d - hi.astype(F32)).astype(BF)], axis=0)

    for copy in near_copy[: HALF - 1]:
        copy.wait_recv()
    prepare_near(0)
    for at in ((0, 1), (0, 3)):
        line[at].wait_recv()
        go(across[at])
    for at in ((1, 0), (3, 0)):
        line[at].wait_recv()
    for at in ((1, 1), (3, 3), (1, 3), (3, 1), (1, 2), (3, 2)):
        go(corner[at])
    for at in ((1, 0), (3, 0)):
        go(across[at])
    line[0, 2].wait_recv()
    go(across[0, 2])
    across[0, 0].wait_recv()
    across[0, 1].wait_recv()
    prepare_far(0)

    later = [corner[2, 1], corner[2, 3], corner[2, 2], across[2, 0]]
    back_copy = [
        send(partial.at[s], landed.at[s], back_s.at[s], back_r.at[s], near_from[s]) for s in range(1, NEAR)
    ]

    def tile(q, slot, slots, fresh):
        rows = pl.ds(pl.multiple_of(q * STEP, STEP), STEP)
        columns = pl.ds(pl.multiple_of(slot * SHARD, slots * SHARD), slots * SHARD)
        power = jnp.dot(far_op[rows, :], near_op[:, columns], preferred_element_type=F32)
        value = jnp.exp2(power)
        high = value.astype(BF)
        low = (value - high.astype(F32)).astype(BF)
        d = dir_op[:, rows]
        a = jnp.dot(d, high, preferred_element_type=F32)
        b = jnp.dot(d[:16], low, preferred_element_type=F32)
        product = a[:16] + (a[16:] + b)
        for s in range(slots):
            piece = product[:, s * SHARD : (s + 1) * SHARD]
            partial[slot + s] = piece + (partial[slot + s] if fresh is False else jnp.where(fresh, 0.0, partial[slot + s]))

    def step(t, carry):
        @pl.when(t == 1)
        def _():
            line[2, 0].wait_recv()
            for copy in later:
                copy.start()
            for copy in near_copy[HALF - 1 :]:
                copy.wait_recv()
            prepare_near(1)

        @pl.when(t == 2)
        def _():
            for at in ((1, 1), (3, 3)):
                corner[at].wait_recv()
                across[at].start()
            for at in ((0, 3), (0, 2), (1, 0), (3, 0), (2, 0)):
                across[at].wait_recv()
            prepare_far(1)

        @pl.when(t == 3)
        def _():
            for at in ((1, 3), (3, 1), (1, 2), (3, 2)):
                corner[at].wait_recv()
                across[at].start()

        @pl.when(t == 4)
        def _():
            for at in ((2, 1), (2, 3), (2, 2)):
                corner[at].wait_recv()
                across[at].start()
            for at in ((1, 1), (3, 3)):
                across[at].wait_recv()
            prepare_far(2)

        @pl.when(t == 5)
        def _():
            for a, b, c in FAR_AT[25:]:
                across[a, b].wait_recv()
            prepare_far(3)

        @pl.when(t == 6)
        def _():
            for s in reversed(range(HALF, NEAR)):
                back_copy[s - 1].start()

        late = t // 4
        q = (1 - late) * (t // 2) + late * (2 + lax.rem(t, 2))
        h = (1 - late) * lax.rem(t, 2) + late * (3 - t // 2)
        tile(q, h * HALF, HALF, t < 2)
        return carry

    lax.fori_loop(0, 7, step, 0)
    for first in (QUARTER, 0):
        tile(3, first, QUARTER, False)
        for k in reversed(range(max(first, 1), first + QUARTER)):
            back_copy[k - 1].start()
    pending.extend(later + [across[at] for at in corner] + back_copy)
    image = partial[0]
    for s in range(1, NEAR):
        back_copy[s - 1].wait_recv()
        image = image + landed[s]
    for load in loads[3:]:
        load.wait()
    d, r = direction[...], res[...]
    image = outscale[0] * image + jitter[...] * d
    terms = jnp.concatenate([r * r, d * image, r * image, image * image, jnp.zeros((64, SHARD), F32)], axis=0)
    dots[0:1, :] = jnp.sum(terms.T, axis=0, keepdims=True)
    slot = gathered.at[pl.ds(me, 1)]
    row = dots.at[pl.ds(0, 1)]
    up = [
        send(row, slot, up_s.at[k], up_r, device((x + k // 8) & 3, (y + k % 8) & 7, 0, 1))
        for k in range(LEADERS)
    ]
    for k in range(1, LEADERS):
        go(up[k])
    down = [
        send(total.at[pl.ds(0, 1)], total.at[pl.ds(0, 1)], down_s.at[k], down_r, device(x, y, k // 2, 1 - k % 2))
        for k in range(1, FAR // 2)
    ]

    @pl.when(leader)
    def _():
        pltpu.make_async_copy(row, slot, up_r).start()

    @pl.when(jnp.logical_not(leader))
    def _():
        up[0].start()
        up[0].wait_send()

    for copy in pending:
        copy.wait_send()

    @pl.when(leader)
    def _():
        pltpu.make_async_copy(gathered, gathered, up_r).wait()
        total[0:1, :] = jnp.sum(gathered[...], axis=0, keepdims=True)
        for copy in down:
            copy.start()

    @pl.when(jnp.logical_not(leader))
    def _():
        down[0].wait_recv()

    sums = total[0:1, :]
    spread = jnp.broadcast_to(sums, (SHARD, SHARD)).T
    rr, dq, rq, qq = [spread[16 * k : 16 * (k + 1)] for k in range(4)]
    alpha = rr / dq
    next_rr = rr + alpha * (alpha * qq - 2.0 * rq)
    result[0:16, :] = image
    result[16:32, :] = alpha
    result[32:48, :] = next_rr / rr
    @pl.when(leader)
    def _():
        for copy in down:
            copy.wait_send()


def per_device(points, lengths, outscale, jitter, sol, res, direction):
    vmem = pl.BlockSpec(memory_space=pltpu.VMEM)
    dma = pltpu.SemaphoreType.DMA
    hbm = pl.BlockSpec(memory_space=pltpu.HBM)
    result = pl.pallas_call(
        kernel,
        out_shape=pltpu.VMEM((48, SHARD), F32),
        in_specs=[hbm] * 6,
        out_specs=vmem,
        scratch_shapes=[
            pltpu.VMEM((16, SHARD), F32),
            pltpu.VMEM((1, 16), F32),
            pltpu.SMEM((1,), F32),
            pltpu.VMEM((1, SHARD), F32),
            pltpu.VMEM((16, SHARD), F32),
            pltpu.VMEM((16, SHARD), F32),
            dma((6,)),
            pltpu.VMEM((NEAR, 16, SHARD), F32),
            pltpu.VMEM((FAR, 32, SHARD), F32),
            pltpu.VMEM((DEPTH, NEAR_PTS), BF),
            pltpu.VMEM((FAR * SHARD, DEPTH), BF),
            pltpu.VMEM((32, FAR * SHARD), BF),
            pltpu.VMEM((NEAR, 16, SHARD), F32),
            pltpu.VMEM((NEAR, 16, SHARD), F32),
            pltpu.VMEM((8, SHARD), F32),
            pltpu.VMEM((DEVICES, SHARD), F32),
            pltpu.VMEM((8, SHARD), F32),
            dma((NEAR,)),
            dma((NEAR,)),
            dma((FAR,)),
            dma((FAR,)),
            dma((NEAR,)),
            dma((NEAR,)),
            dma((LEADERS,)),
            dma,
            dma((FAR // 2,)),
            dma,
        ],
        compiler_params=pltpu.CompilerParams(
            collective_id=0, has_side_effects=True, vmem_limit_bytes=63 * 2**20
        ),
        name="cg_step",
    )(
        points.T,
        lengths.reshape(1, 16),
        outscale,
        jitter.reshape(1, SHARD),
        res.T,
        direction.T,
    )
    image, alpha, beta = [result[16 * k : 16 * (k + 1)].T for k in range(3)]
    new_res = res - alpha * image
    return sol + alpha * direction, new_res, new_res + beta * direction


def solution(mesh):
    rows = P(("row", "col"), None)
    return jax.shard_map(
        per_device,
        mesh=mesh,
        in_specs=(rows, P(), P(), P(("row", "col")), rows, rows, rows),
        out_specs=(rows, rows, rows),
        check_vma=False,
    )
```

```python
import math

import jax
import jax.numpy as jnp
from jax import lax
from jax.experimental import pallas as pl
from jax.experimental.pallas import tpu as pltpu
from jax.sharding import PartitionSpec as P

MESH = pl.DeviceIdType.MESH
BF = jnp.bfloat16
F32 = jnp.float32
LOG2E = math.log2(math.e)
DEPTH = 128
NEAR = 16
FAR = 32
SHARD = 128
NEAR_PTS = NEAR * SHARD
CHUNK = 8
LEADERS = 32
DEVICES = 512
HALF = NEAR // 2
QUARTER = HALF // 2
STEP = CHUNK * SHARD
NEAR_AT = (
    (0, 0), (1, 0), (7, 0), (0, 1), (1, 1), (7, 1), (2, 0), (6, 0),
    (3, 0), (5, 0), (2, 1), (6, 1), (4, 0), (3, 1), (5, 1), (4, 1),
)
FAR_AT = (
    (0, 0, 0), (0, 1, 0), (0, 3, 0), (1, 0, 0), (3, 0, 0), (0, 2, 0), (0, 0, 1), (0, 1, 1),
    (0, 3, 1), (0, 2, 1), (1, 0, 1), (3, 0, 1), (2, 0, 0), (2, 0, 1), (1, 1, 0), (3, 3, 0),
    (1, 3, 0), (3, 1, 0), (1, 2, 0), (3, 2, 0), (1, 1, 1), (3, 3, 1), (2, 1, 0), (2, 3, 0),
    (2, 2, 0), (1, 3, 1), (3, 1, 1), (1, 2, 1), (3, 2, 1), (2, 1, 1), (2, 3, 1), (2, 2, 1),
)
SLOT = {at: k for k, at in enumerate(FAR_AT)}
LINES = ((0, 1), (0, 3), (1, 0), (3, 0), (0, 2), (2, 0))

def split3(x):
    hi = x.astype(BF)
    rest = x - hi.astype(F32)
    mid = rest.astype(BF)
    low = (rest - mid.astype(F32)).astype(BF)
    return hi, mid, low


def augment(u, near):
    hi, mid, low = split3(u)
    half = -0.5 * jnp.sum(u * u, axis=0, keepdims=True)
    h0, h1, h2 = [part.astype(F32) for part in split3(half)]
    row = lax.broadcasted_iota(jnp.int32, u.shape, 0)
    if near:
        ones = jnp.where((row >= 3) & (row < 6), 1.0, 0.0)
        tail = jnp.where(row == 0, h0, jnp.where(row == 1, h1, jnp.where(row == 2, h2, ones)))
        parts = [hi, hi, mid, mid, hi, low]
    else:
        ones = jnp.where(row < 3, 1.0, 0.0)
        tail = jnp.where(row == 3, h0, jnp.where(row == 4, h1, jnp.where(row == 5, h2, ones)))
        parts = [hi, mid, hi, mid, low, hi]
    return jnp.concatenate(parts + [tail.astype(BF), jnp.zeros_like(hi)], axis=0)


def place():
    r, c = lax.axis_index("row"), lax.axis_index("col")
    x, z, core = c >> 2, r >> 2, r & 1
    y = (c & 3) * 2 + ((r >> 1) & 1)
    return x, y, z, core


def device(x, y, z, core):
    return (z * 4 + (y & 1) * 2 + core, x * 4 + (y >> 1))


def kernel(
    points_hbm,
    lengths_hbm,
    outscale_hbm,
    jitter_hbm,
    res_hbm,
    direction_hbm,
    result,
    points,
    lengths,
    outscale,
    jitter,
    res,
    direction,
    load_sem,
    near,
    far,
    near_op,
    far_op,
    dir_op,
    partial,
    landed,
    dots,
    gathered,
    total,
    near_s,
    near_r,
    far_s,
    far_r,
    back_s,
    back_r,
    up_s,
    up_r,
    down_s,
    down_r,
):
    x, y, z, core = place()

    def near_peer(slot, sign):
        dy, dz = NEAR_AT[slot]
        return device(x, (y + sign * dy) & 7, z ^ dz, core)

    def far_peer(a, b, c):
        return device((x + b) & 3, y, (z + 2 * a) & 7, core ^ c)

    def send(src, dst, ss, rs, peer):
        return pltpu.make_async_remote_copy(
            src_ref=src, dst_ref=dst, send_sem=ss, recv_sem=rs, device_id=peer, device_id_type=MESH
        )

    near_to = [near_peer(s, 1) for s in range(NEAR)]
    near_from = [near_peer(s, -1) for s in range(NEAR)]
    line_to = [far_peer(a, b, 0) for a, b in LINES]
    mate = far_peer(0, 0, 1)
    leader = (z == 0) & (core == 1)
    me = (z * 2 + core) * 32 + x * 8 + y

    barrier = pltpu.get_barrier_semaphore()
    greeted = line_to + near_to[:0:-1] + [mate]
    for peer in greeted:
        pl.semaphore_signal(barrier, inc=1, device_id=peer, device_id_type=MESH)

    loads = [
        pltpu.make_async_copy(src, dst, load_sem.at[k])
        for k, (src, dst) in enumerate(
            (
                (points_hbm, points),
                (lengths_hbm, lengths),
                (direction_hbm, direction),
                (outscale_hbm, outscale),
                (jitter_hbm, jitter),
                (res_hbm, res),
            )
        )
    ]
    for load in loads:
        load.start()
    pending = []

    def go(copy):
        copy.start()
        pending.append(copy)

    for load in loads[:3]:
        load.wait()

    eye = lax.broadcasted_iota(jnp.int32, (16, 16), 0) == lax.broadcasted_iota(jnp.int32, (16, 16), 1)
    column = jnp.sum(jnp.where(eye, jnp.broadcast_to(lengths[...], (16, 16)), 0.0), axis=1, keepdims=True)
    mine = points[...] * (math.sqrt(LOG2E) / column)
    near[0] = mine
    far[0, :16] = mine
    far[0, 16:] = direction[...]

    pl.semaphore_wait(barrier, len(greeted))

    def far_copy(source, at, peer):
        k = SLOT[at]
        return send(far.at[SLOT[source]], far.at[k], far_s.at[k], far_r.at[k], peer)

    line = {(a, b): far_copy((0, 0, 0), (a, b, 0), peer) for (a, b), peer in zip(LINES, line_to)}
    corner = {
        (a, b): far_copy((a, 0, 0), (a, b, 0), far_peer(0, b, 0)) for a in (1, 2, 3) for b in (1, 2, 3)
    }
    across = {(a, b): far_copy((a, b, 0), (a, b, 1), mate) for a in range(4) for b in range(4)}
    near_copy = [
        send(near.at[0], near.at[s], near_s.at[s], near_r.at[s], near_to[s]) for s in range(1, NEAR)
    ]
    for s in range(1, HALF):
        go(near_copy[s - 1])
    for at in LINES:
        go(line[at])
    go(across[0, 0])
    for s in reversed(range(HALF, NEAR)):
        go(near_copy[s - 1])

    def prepare_near(h):
        for s in range(h * HALF, h * HALF + HALF):
            near_op[:, s * SHARD : (s + 1) * SHARD] = augment(near[s], True)

    def prepare_far(q):
        for k in range(q * CHUNK, q * CHUNK + CHUNK):
            here = slice(k * SHARD, (k + 1) * SHARD)
            far_op[here, :] = augment(far[k, :16], False).T
            d = far[k, 16:]
            hi = d.astype(BF)
            dir_op[:, here] = jnp.concatenate([hi, (d - hi.astype(F32)).astype(BF)], axis=0)

    for copy in near_copy[: HALF - 1]:
        copy.wait_recv()
    prepare_near(0)
    for at in ((0, 1), (0, 3)):
        line[at].wait_recv()
        go(across[at])
    for at in ((1, 0), (3, 0)):
        line[at].wait_recv()
    for at in ((1, 1), (3, 3), (1, 3), (3, 1), (1, 2), (3, 2)):
        go(corner[at])
    for at in ((1, 0), (3, 0)):
        go(across[at])
    line[0, 2].wait_recv()
    go(across[0, 2])
    across[0, 0].wait_recv()
    across[0, 1].wait_recv()
    prepare_far(0)

    later = [corner[2, 1], corner[2, 3], corner[2, 2], across[2, 0]]
    back_copy = [
        send(partial.at[s], landed.at[s], back_s.at[s], back_r.at[s], near_from[s]) for s in range(1, NEAR)
    ]

    def tile(q, slot, slots, fresh):
        rows = pl.ds(pl.multiple_of(q * STEP, STEP), STEP)
        columns = pl.ds(pl.multiple_of(slot * SHARD, slots * SHARD), slots * SHARD)
        power = jnp.dot(far_op[rows, :], near_op[:, columns], preferred_element_type=F32)
        value = jnp.exp2(power)
        high = value.astype(BF)
        low = (value - high.astype(F32)).astype(BF)
        d = dir_op[:, rows]
        a = jnp.dot(d, high, preferred_element_type=F32)
        b = jnp.dot(d[:16], low, preferred_element_type=F32)
        product = a[:16] + (a[16:] + b)
        for s in range(slots):
            piece = product[:, s * SHARD : (s + 1) * SHARD]
            partial[slot + s] = piece + (partial[slot + s] if fresh is False else jnp.where(fresh, 0.0, partial[slot + s]))

    def step(t, carry):
        @pl.when(t == 1)
        def _():
            line[2, 0].wait_recv()
            for copy in later:
                copy.start()
            for copy in near_copy[HALF - 1 :]:
                copy.wait_recv()
            prepare_near(1)

        @pl.when(t == 2)
        def _():
            for at in ((1, 1), (3, 3)):
                corner[at].wait_recv()
                across[at].start()
            for at in ((0, 3), (0, 2), (1, 0), (3, 0), (2, 0)):
                across[at].wait_recv()
            prepare_far(1)

        @pl.when(t == 3)
        def _():
            for at in ((1, 3), (3, 1), (1, 2), (3, 2)):
                corner[at].wait_recv()
                across[at].start()

        @pl.when(t == 4)
        def _():
            for at in ((2, 1), (2, 3), (2, 2)):
                corner[at].wait_recv()
                across[at].start()
            for at in ((1, 1), (3, 3)):
                across[at].wait_recv()
            prepare_far(2)

        @pl.when(t == 5)
        def _():
            for a, b, c in FAR_AT[25:]:
                across[a, b].wait_recv()
            prepare_far(3)

        @pl.when(t == 6)
        def _():
            for s in reversed(range(HALF, NEAR)):
                back_copy[s - 1].start()

        late = t // 4
        q = (1 - late) * (t // 2) + late * (2 + lax.rem(t, 2))
        h = (1 - late) * lax.rem(t, 2) + late * (3 - t // 2)
        tile(q, h * HALF, HALF, t < 2)
        return carry

    lax.fori_loop(0, 7, step, 0)
    for first in (QUARTER, 0):
        tile(3, first, QUARTER, False)
        for k in reversed(range(max(first, 1), first + QUARTER)):
            back_copy[k - 1].start()
    pending.extend(later + [across[at] for at in corner] + back_copy)
    for load in loads[3:]:
        load.wait()
    d, r = direction[...], res[...]
    noise = jitter[...] * d
    image = partial[0]
    for s in (*range(HALF, NEAR), *range(QUARTER, HALF), *range(1, QUARTER)):
        back_copy[s - 1].wait_recv()
        image = image + landed[s]
    image = outscale[0] * image + noise
    terms = jnp.concatenate([r * r, d * image, r * image, image * image, jnp.zeros((64, SHARD), F32)], axis=0)
    dots[0:1, :] = jnp.sum(terms.T, axis=0, keepdims=True)
    slot = gathered.at[pl.ds(me, 1)]
    row = dots.at[pl.ds(0, 1)]
    up = [
        send(row, slot, up_s.at[k], up_r, device((x + k // 8) & 3, (y + k % 8) & 7, 0, 1))
        for k in range(LEADERS)
    ]
    for k in range(1, LEADERS):
        go(up[k])
    down = [
        send(total.at[pl.ds(0, 1)], total.at[pl.ds(0, 1)], down_s.at[k], down_r, device(x, y, k // 2, 1 - k % 2))
        for k in range(1, FAR // 2)
    ]

    @pl.when(leader)
    def _():
        pltpu.make_async_copy(row, slot, up_r).start()

    @pl.when(jnp.logical_not(leader))
    def _():
        up[0].start()
        up[0].wait_send()

    for copy in pending:
        copy.wait_send()

    @pl.when(leader)
    def _():
        pltpu.make_async_copy(gathered, gathered, up_r).wait()
        total[0:1, :] = jnp.sum(gathered[...], axis=0, keepdims=True)
        for copy in down:
            copy.start()

    @pl.when(jnp.logical_not(leader))
    def _():
        down[0].wait_recv()

    sums = total[0:1, :]
    spread = jnp.broadcast_to(sums, (SHARD, SHARD)).T
    rr, dq, rq, qq = [spread[16 * k : 16 * (k + 1)] for k in range(4)]
    alpha = rr / dq
    next_rr = rr + alpha * (alpha * qq - 2.0 * rq)
    result[0:16, :] = image
    result[16:32, :] = alpha
    result[32:48, :] = next_rr / rr
    @pl.when(leader)
    def _():
        for copy in down:
            copy.wait_send()


def per_device(points, lengths, outscale, jitter, sol, res, direction):
    vmem = pl.BlockSpec(memory_space=pltpu.VMEM)
    dma = pltpu.SemaphoreType.DMA
    hbm = pl.BlockSpec(memory_space=pltpu.HBM)
    result = pl.pallas_call(
        kernel,
        out_shape=pltpu.VMEM((48, SHARD), F32),
        in_specs=[hbm] * 6,
        out_specs=vmem,
        scratch_shapes=[
            pltpu.VMEM((16, SHARD), F32),
            pltpu.VMEM((1, 16), F32),
            pltpu.SMEM((1,), F32),
            pltpu.VMEM((1, SHARD), F32),
            pltpu.VMEM((16, SHARD), F32),
            pltpu.VMEM((16, SHARD), F32),
            dma((6,)),
            pltpu.VMEM((NEAR, 16, SHARD), F32),
            pltpu.VMEM((FAR, 32, SHARD), F32),
            pltpu.VMEM((DEPTH, NEAR_PTS), BF),
            pltpu.VMEM((FAR * SHARD, DEPTH), BF),
            pltpu.VMEM((32, FAR * SHARD), BF),
            pltpu.VMEM((NEAR, 16, SHARD), F32),
            pltpu.VMEM((NEAR, 16, SHARD), F32),
            pltpu.VMEM((8, SHARD), F32),
            pltpu.VMEM((DEVICES, SHARD), F32),
            pltpu.VMEM((8, SHARD), F32),
            dma((NEAR,)),
            dma((NEAR,)),
            dma((FAR,)),
            dma((FAR,)),
            dma((NEAR,)),
            dma((NEAR,)),
            dma((LEADERS,)),
            dma,
            dma((FAR // 2,)),
            dma,
        ],
        compiler_params=pltpu.CompilerParams(
            collective_id=0, has_side_effects=True, vmem_limit_bytes=63 * 2**20
        ),
        name="cg_step",
    )(
        points.T,
        lengths.reshape(1, 16),
        outscale,
        jitter.reshape(1, SHARD),
        res.T,
        direction.T,
    )
    image, alpha, beta = [result[16 * k : 16 * (k + 1)].T for k in range(3)]
    new_res = res - alpha * image
    return sol + alpha * direction, new_res, new_res + beta * direction


def solution(mesh):
    rows = P(("row", "col"), None)
    return jax.shard_map(
        per_device,
        mesh=mesh,
        in_specs=(rows, P(), P(), P(("row", "col")), rows, rows, rows),
        out_specs=(rows, rows, rows),
        check_vma=False,
    )
```

```python
import math

import jax
import jax.numpy as jnp
from jax import lax
from jax.experimental import pallas as pl
from jax.experimental.pallas import tpu as pltpu
from jax.sharding import PartitionSpec as P

MESH = pl.DeviceIdType.MESH
BF = jnp.bfloat16
F32 = jnp.float32
LOG2E = math.log2(math.e)
DEPTH = 128
NEAR = 16
FAR = 32
SHARD = 128
NEAR_PTS = NEAR * SHARD
CHUNK = 8
LEADERS = 32
DEVICES = 512
HALF = NEAR // 2
QUARTER = HALF // 2
STEP = CHUNK * SHARD
NEAR_AT = (
    (0, 0), (1, 0), (7, 0), (0, 1), (1, 1), (7, 1), (2, 0), (6, 0),
    (3, 0), (5, 0), (2, 1), (6, 1), (4, 0), (3, 1), (5, 1), (4, 1),
)
FAR_AT = (
    (0, 0, 0), (0, 1, 0), (0, 3, 0), (1, 0, 0), (3, 0, 0), (0, 2, 0), (0, 0, 1), (0, 1, 1),
    (0, 3, 1), (0, 2, 1), (1, 0, 1), (3, 0, 1), (2, 0, 0), (2, 0, 1), (1, 1, 0), (3, 3, 0),
    (1, 3, 0), (3, 1, 0), (1, 2, 0), (3, 2, 0), (1, 1, 1), (3, 3, 1), (2, 1, 0), (2, 3, 0),
    (2, 2, 0), (1, 3, 1), (3, 1, 1), (1, 2, 1), (3, 2, 1), (2, 1, 1), (2, 3, 1), (2, 2, 1),
)
SLOT = {at: k for k, at in enumerate(FAR_AT)}
LINES = ((0, 1), (0, 3), (1, 0), (3, 0), (0, 2), (2, 0))

def split3(x):
    hi = x.astype(BF)
    rest = x - hi.astype(F32)
    mid = rest.astype(BF)
    low = (rest - mid.astype(F32)).astype(BF)
    return hi, mid, low


def augment(u, near):
    hi, mid, low = split3(u)
    half = -0.5 * jnp.sum(u * u, axis=0, keepdims=True)
    h0, h1, h2 = [part.astype(F32) for part in split3(half)]
    row = lax.broadcasted_iota(jnp.int32, u.shape, 0)
    if near:
        ones = jnp.where((row >= 3) & (row < 6), 1.0, 0.0)
        tail = jnp.where(row == 0, h0, jnp.where(row == 1, h1, jnp.where(row == 2, h2, ones)))
        parts = [hi, hi, mid, mid, hi, low]
    else:
        ones = jnp.where(row < 3, 1.0, 0.0)
        tail = jnp.where(row == 3, h0, jnp.where(row == 4, h1, jnp.where(row == 5, h2, ones)))
        parts = [hi, mid, hi, mid, low, hi]
    return jnp.concatenate(parts + [tail.astype(BF), jnp.zeros_like(hi)], axis=0)


def place():
    r, c = lax.axis_index("row"), lax.axis_index("col")
    x, z, core = c >> 2, r >> 2, r & 1
    y = (c & 3) * 2 + ((r >> 1) & 1)
    return x, y, z, core


def device(x, y, z, core):
    return (z * 4 + (y & 1) * 2 + core, x * 4 + (y >> 1))


def kernel(
    points_hbm,
    lengths_hbm,
    outscale_hbm,
    jitter_hbm,
    res_hbm,
    direction_hbm,
    result,
    points,
    lengths,
    outscale,
    jitter,
    res,
    direction,
    load_sem,
    near,
    far,
    near_op,
    far_op,
    dir_op,
    partial,
    landed,
    dots,
    gathered,
    total,
    near_s,
    near_r,
    far_s,
    far_r,
    back_s,
    back_r,
    up_s,
    up_r,
    down_s,
    down_r,
):
    x, y, z, core = place()

    def near_peer(slot, sign):
        dy, dz = NEAR_AT[slot]
        return device(x, (y + sign * dy) & 7, z ^ dz, core)

    def far_peer(a, b, c):
        return device((x + b) & 3, y, (z + 2 * a) & 7, core ^ c)

    def send(src, dst, ss, rs, peer):
        return pltpu.make_async_remote_copy(
            src_ref=src, dst_ref=dst, send_sem=ss, recv_sem=rs, device_id=peer, device_id_type=MESH
        )

    near_to = [near_peer(s, 1) for s in range(NEAR)]
    near_from = [near_peer(s, -1) for s in range(NEAR)]
    line_to = [far_peer(a, b, 0) for a, b in LINES]
    mate = far_peer(0, 0, 1)
    leader = (z == 0) & (core == 1)
    me = (z * 2 + core) * 32 + x * 8 + y

    barrier = pltpu.get_barrier_semaphore()
    greeted = line_to + near_to[:0:-1] + [mate]
    for peer in greeted:
        pl.semaphore_signal(barrier, inc=1, device_id=peer, device_id_type=MESH)

    loads = [
        pltpu.make_async_copy(src, dst, load_sem.at[k])
        for k, (src, dst) in enumerate(
            (
                (points_hbm, points),
                (lengths_hbm, lengths),
                (direction_hbm, direction),
                (outscale_hbm, outscale),
                (jitter_hbm, jitter),
                (res_hbm, res),
            )
        )
    ]
    for load in loads:
        load.start()
    pending = []

    def go(copy):
        copy.start()
        pending.append(copy)

    for load in loads[:3]:
        load.wait()

    eye = lax.broadcasted_iota(jnp.int32, (16, 16), 0) == lax.broadcasted_iota(jnp.int32, (16, 16), 1)
    column = jnp.sum(jnp.where(eye, jnp.broadcast_to(lengths[...], (16, 16)), 0.0), axis=1, keepdims=True)
    mine = points[...] * (math.sqrt(LOG2E) / column)
    near[0] = mine
    far[0, :16] = mine
    far[0, 16:] = direction[...]

    pl.semaphore_wait(barrier, len(greeted))

    def far_copy(source, at, peer):
        k = SLOT[at]
        return send(far.at[SLOT[source]], far.at[k], far_s.at[k], far_r.at[k], peer)

    line = {(a, b): far_copy((0, 0, 0), (a, b, 0), peer) for (a, b), peer in zip(LINES, line_to)}
    corner = {
        (a, b): far_copy((a, 0, 0), (a, b, 0), far_peer(0, b, 0)) for a in (1, 2, 3) for b in (1, 2, 3)
    }
    across = {(a, b): far_copy((a, b, 0), (a, b, 1), mate) for a in range(4) for b in range(4)}
    near_copy = [
        send(near.at[0], near.at[s], near_s.at[s], near_r.at[s], near_to[s]) for s in range(1, NEAR)
    ]
    for s in range(1, HALF):
        go(near_copy[s - 1])
    for at in LINES:
        go(line[at])
    go(across[0, 0])
    for s in reversed(range(HALF, NEAR)):
        go(near_copy[s - 1])

    def prepare_near(h):
        for s in range(h * HALF, h * HALF + HALF):
            near_op[:, s * SHARD : (s + 1) * SHARD] = augment(near[s], True)

    def prepare_far(q):
        for k in range(q * CHUNK, q * CHUNK + CHUNK):
            here = slice(k * SHARD, (k + 1) * SHARD)
            far_op[here, :] = augment(far[k, :16], False).T
            d = far[k, 16:]
            hi = d.astype(BF)
            dir_op[:, here] = jnp.concatenate([hi, (d - hi.astype(F32)).astype(BF)], axis=0)

    for copy in near_copy[: HALF - 1]:
        copy.wait_recv()
    prepare_near(0)
    for at in ((0, 1), (0, 3)):
        line[at].wait_recv()
        go(across[at])
    for at in ((1, 0), (3, 0)):
        line[at].wait_recv()
    for at in ((1, 1), (3, 3), (1, 3), (3, 1), (1, 2), (3, 2)):
        go(corner[at])
    for at in ((1, 0), (3, 0)):
        go(across[at])
    line[0, 2].wait_recv()
    go(across[0, 2])
    across[0, 0].wait_recv()
    across[0, 1].wait_recv()
    prepare_far(0)

    later = [corner[2, 1], corner[2, 3], corner[2, 2], across[2, 0]]
    back_copy = [
        send(partial.at[s], landed.at[s], back_s.at[s], back_r.at[s], near_from[s]) for s in range(1, NEAR)
    ]

    def tile(q, slot, slots, fresh):
        rows = pl.ds(pl.multiple_of(q * STEP, STEP), STEP)
        columns = pl.ds(pl.multiple_of(slot * SHARD, slots * SHARD), slots * SHARD)
        power = jnp.dot(far_op[rows, :], near_op[:, columns], preferred_element_type=F32)
        value = jnp.exp2(power)
        high = value.astype(BF)
        low = (value - high.astype(F32)).astype(BF)
        d = dir_op[:, rows]
        a = jnp.dot(d, high, preferred_element_type=F32)
        b = jnp.dot(d[:16], low, preferred_element_type=F32)
        product = a[:16] + (a[16:] + b)
        for s in range(slots):
            piece = product[:, s * SHARD : (s + 1) * SHARD]
            partial[slot + s] = piece + (partial[slot + s] if fresh is False else jnp.where(fresh, 0.0, partial[slot + s]))

    def step(t, carry):
        @pl.when(t == 1)
        def _():
            line[2, 0].wait_recv()
            for copy in later:
                copy.start()
            for copy in near_copy[HALF - 1 :]:
                copy.wait_recv()
            prepare_near(1)

        @pl.when(t == 2)
        def _():
            for at in ((1, 1), (3, 3)):
                corner[at].wait_recv()
                across[at].start()
            for at in ((0, 3), (0, 2), (1, 0), (3, 0), (2, 0)):
                across[at].wait_recv()
            prepare_far(1)

        @pl.when(t == 3)
        def _():
            for at in ((1, 3), (3, 1), (1, 2), (3, 2)):
                corner[at].wait_recv()
                across[at].start()

        @pl.when(t == 4)
        def _():
            for at in ((2, 1), (2, 3), (2, 2)):
                corner[at].wait_recv()
                across[at].start()
            for at in ((1, 1), (3, 3)):
                across[at].wait_recv()
            prepare_far(2)

        @pl.when(t == 5)
        def _():
            for a, b, c in FAR_AT[25:]:
                across[a, b].wait_recv()
            prepare_far(3)

        @pl.when(t == 6)
        def _():
            for s in reversed(range(HALF, NEAR)):
                back_copy[s - 1].start()

        late = t // 4
        q = (1 - late) * (t // 2) + late * (2 + lax.rem(t, 2))
        h = (1 - late) * lax.rem(t, 2) + late * (3 - t // 2)
        tile(q, h * HALF, HALF, t < 2)
        return carry

    lax.fori_loop(0, 7, step, 0)
    for first in (QUARTER, 0):
        tile(3, first, QUARTER, False)
        for k in reversed(range(max(first, 1), first + QUARTER)):
            back_copy[k - 1].start()
    pending.extend(later + [across[at] for at in corner] + back_copy)
    for load in loads[3:]:
        load.wait()
    d, r = direction[...], res[...]
    noise = jitter[...] * d
    image = partial[0]
    for s in (*range(HALF, NEAR), *range(QUARTER, HALF), *range(1, QUARTER)):
        back_copy[s - 1].wait_recv()
        image = image + landed[s]
    image = outscale[0] * image + noise
    terms = jnp.concatenate([r * r, d * image, r * image, image * image, jnp.zeros((64, SHARD), F32)], axis=0)
    dots[0:1, :] = jnp.sum(terms.T, axis=0, keepdims=True)
    slot = gathered.at[pl.ds(me, 1)]
    row = dots.at[pl.ds(0, 1)]
    up = [
        send(row, slot, up_s.at[k], up_r, device((x + k // 8) & 3, (y + k % 8) & 7, 0, 1))
        for k in range(LEADERS)
    ]
    for k in sorted(range(1, LEADERS), key=lambda k: -min(k // 8, 4 - k // 8) - min(k % 8, 8 - k % 8)):
        go(up[k])
    result[0:16, :] = image
    down = [
        send(total.at[pl.ds(0, 1)], total.at[pl.ds(0, 1)], down_s.at[k], down_r, device(x, y, k // 2, 1 - k % 2))
        for k in range(1, FAR // 2)
    ]

    @pl.when(leader)
    def _():
        pltpu.make_async_copy(row, slot, up_r).start()

    @pl.when(jnp.logical_not(leader))
    def _():
        up[0].start()
        up[0].wait_send()

    for copy in pending:
        copy.wait_send()

    @pl.when(leader)
    def _():
        pltpu.make_async_copy(gathered, gathered, up_r).wait()
        total[0:1, :] = jnp.sum(gathered[...], axis=0, keepdims=True)
        for copy in down:
            copy.start()

    @pl.when(jnp.logical_not(leader))
    def _():
        down[0].wait_recv()

    sums = total[0:1, :]
    spread = jnp.broadcast_to(sums, (SHARD, SHARD)).T
    rr, dq, rq, qq = [spread[16 * k : 16 * (k + 1)] for k in range(4)]
    alpha = rr / dq
    next_rr = rr + alpha * (alpha * qq - 2.0 * rq)
    result[16:32, :] = alpha
    result[32:48, :] = next_rr / rr
    @pl.when(leader)
    def _():
        for copy in down:
            copy.wait_send()


def per_device(points, lengths, outscale, jitter, sol, res, direction):
    vmem = pl.BlockSpec(memory_space=pltpu.VMEM)
    dma = pltpu.SemaphoreType.DMA
    hbm = pl.BlockSpec(memory_space=pltpu.HBM)
    result = pl.pallas_call(
        kernel,
        out_shape=pltpu.VMEM((48, SHARD), F32),
        in_specs=[hbm] * 6,
        out_specs=vmem,
        scratch_shapes=[
            pltpu.VMEM((16, SHARD), F32),
            pltpu.VMEM((1, 16), F32),
            pltpu.SMEM((1,), F32),
            pltpu.VMEM((1, SHARD), F32),
            pltpu.VMEM((16, SHARD), F32),
            pltpu.VMEM((16, SHARD), F32),
            dma((6,)),
            pltpu.VMEM((NEAR, 16, SHARD), F32),
            pltpu.VMEM((FAR, 32, SHARD), F32),
            pltpu.VMEM((DEPTH, NEAR_PTS), BF),
            pltpu.VMEM((FAR * SHARD, DEPTH), BF),
            pltpu.VMEM((32, FAR * SHARD), BF),
            pltpu.VMEM((NEAR, 16, SHARD), F32),
            pltpu.VMEM((NEAR, 16, SHARD), F32),
            pltpu.VMEM((8, SHARD), F32),
            pltpu.VMEM((DEVICES, SHARD), F32),
            pltpu.VMEM((8, SHARD), F32),
            dma((NEAR,)),
            dma((NEAR,)),
            dma((FAR,)),
            dma((FAR,)),
            dma((NEAR,)),
            dma((NEAR,)),
            dma((LEADERS,)),
            dma,
            dma((FAR // 2,)),
            dma,
        ],
        compiler_params=pltpu.CompilerParams(
            collective_id=0, has_side_effects=True, vmem_limit_bytes=63 * 2**20
        ),
        name="cg_step",
    )(
        points.T,
        lengths.reshape(1, 16),
        outscale,
        jitter.reshape(1, SHARD),
        res.T,
        direction.T,
    )
    image, alpha, beta = [result[16 * k : 16 * (k + 1)].T for k in range(3)]
    new_res = res - alpha * image
    return sol + alpha * direction, new_res, new_res + beta * direction


def solution(mesh):
    rows = P(("row", "col"), None)
    return jax.shard_map(
        per_device,
        mesh=mesh,
        in_specs=(rows, P(), P(), P(("row", "col")), rows, rows, rows),
        out_specs=(rows, rows, rows),
        check_vma=False,
    )
```
